32 devices in a mesh: ctx: 8 (over y, x, core), req: 4 (over z).
Axes of the slice: x: 2, y: 2, z: 4, core: 2. Of those that a mesh axis runs over, the one named last changes fastest.
Arguments:
- queries: bfloat16 [2048, 2048], P(('ctx', 'req')), may hold values from -20 to 20
- q_pos: int32 [2048], P(('ctx', 'req')), may hold values from 1 to 18431
- req_of: int32 [2048, 1], P(('ctx', 'req')), may hold values from 0 to 3; in each aligned block of 64 rows (0 to 63, 64 to 127, ...) at most 20 rows name the same one
- cache: bfloat16 [4, 18432, 256], P('req', 'ctx'), may hold values from -6 to 6
- cache_len: int32 [4], replicated, may hold values from 2 to 18432
Outputs:
- attended: bfloat16 [2048, 2048], P(('ctx', 'req'))
The draws below stay inside these ranges and needn't reach their ends.
Inputs may be any that keep to these rules, and one draw needn't show every extreme that they name: `req_of`: no more than 20 of one device's 64 tokens name the same request, and some device's tokens reach 20 for some request.
All inputs are finite; a program needn't handle non-finite values.
Results may differ from the reference program's by a relative error of at most 0.006.
Values may be sent and summed in bfloat16 or wider, within the bound.
No kernel may reach another device: no remote copies, remote signals or barrier semaphores. Data moves between devices by JAX's collectives and lax.ppermute only.
A program may use at most 128 MiB of HBM per device.

```python
import math
import jax
import jax.numpy as jnp
import numpy as np
from jax import lax

H = 16
HD = 128
TOK_DEV = 64
CTX_DEV = 2304
REQS = 4
CTX_LEN = 18432
TOKENS = 2048
CAP = 20
N_CTX = 8


def draw_queries(key, part):
    key = jax.random.fold_in(key, 11)
    key_a = jax.random.fold_in(key, 0)
    base = jnp.clip(jax.random.normal(key_a, (TOKENS, H, HD), jnp.float32), -6.0, 6.0)
    return base.reshape(TOKENS, H * HD).astype(jnp.bfloat16)


def draw_cache(key, part):
    key = jax.random.fold_in(key, 12)
    base = jnp.clip(jax.random.normal(key, (REQS, CTX_LEN, 2 * HD), jnp.float32), -6.0, 6.0)
    return base.astype(jnp.bfloat16)


def set_ends(array, own_key, low, high):
    longest = array.shape.index(max(array.shape))
    spots = []
    for shift in (0, 1):
        where = [jax.random.randint(jax.random.fold_in(own_key, axis), (), 0, length) for axis, length in enumerate(array.shape)]
        where[longest] = (where[longest] + shift) % array.shape[longest]
        spots.append(tuple(where))
    return array.at[spots[0]].set(low).at[spots[1]].set(high)


def routed_block(key, own, number, rows, number_of, top, bound, lean):
    order = jax.random.permutation(key, number_of)
    packed, common = load_shares(number_of, rows * top, bound, lean, True), load_shares(number_of, rows * top, bound, lean, False)
    places = jnp.arange(number_of)

    def named(lengths, turn):
        used = int((lengths > 0).sum())
        fixed = max(1, used // 4)
        shifted = fixed + (places - fixed + turn * (used - fixed)) % max(1, number_of - fixed)
        return jnp.zeros((number_of,), jnp.int32).at[order[jnp.where(places < fixed, places, shifted)]].set(jnp.asarray(lengths, jnp.int32))

    lengths = jnp.where(number % 4 == 0, named(packed, number // 4), named(common, number - number // 4 - 1))
    mixed = jax.random.permutation(jax.random.fold_in(own, 3), number_of)
    source_of, sink = mixed[0:number_of // 2 * 2:2], mixed[1:number_of // 2 * 2:2]
    room = jnp.minimum(lengths[source_of] - 1, bound - lengths[sink]) // 2
    room = jnp.where((source_of == order[0]) | (sink == order[0]) | (lengths[sink] == 0), 0, jnp.maximum(room, 0))
    shifted = jax.random.randint(jax.random.fold_in(own, 4), (number_of // 2,), 0, 1 << 20) % (room + 1)
    lengths = lengths.at[source_of].add(-shifted).at[sink].add(shifted)
    members = jnp.searchsorted(jnp.cumsum(lengths), jnp.arange(rows * top), side="right").astype(jnp.int32)
    listing = members.reshape(top, rows).T
    listing = listing[jax.random.permutation(jax.random.fold_in(own, 1), rows)]
    turn = jax.random.randint(jax.random.fold_in(own, 2), (rows, 1), 0, top)
    return jnp.take_along_axis(listing, (jnp.arange(top)[None, :] + turn) % top, axis=1)


def load_shares(number_of, total, bound, slope, full):
    weights = [(1 << 20) // math.isqrt(standing ** slope) + 1 for standing in range(1, number_of + 1)]
    largest = bound if full else min(bound, max(-(-total // number_of), total * weights[0] // sum(weights)))
    least = 1 if total - largest >= number_of - 1 else 0
    counts, surplus = [largest] + [least] * (number_of - 1), total - largest - least * (number_of - 1)
    while surplus > 0:
        free = [i for i in range(1, number_of) if counts[i] < largest] or [i for i in range(1, number_of) if counts[i] < bound]
        whole, remaining = sum([weights[i] for i in free]), surplus
        for i in free:
            addition = min(bound - counts[i], max(1, remaining * weights[i] // whole), surplus)
            counts[i] = counts[i] + addition
            surplus = surplus - addition
    return np.array(counts)


def setup_inputs(seed: int = 0) -> dict:
    splits = jax.random.split(jax.random.key(seed), 6)
    queries = draw_queries(jax.random.fold_in(splits[5], 71), 0)
    q_pos = set_ends(jax.random.randint(splits[1], (TOKENS,), 1, CTX_LEN), jax.random.fold_in(splits[1], 1), 1, CTX_LEN - 1).astype(jnp.int32)
    req_of_keys = jax.random.split(jax.random.fold_in(splits[2], 1), TOKENS // TOK_DEV)
    req_of_turns = jax.random.permutation(jax.random.fold_in(splits[2], 3), TOKENS // TOK_DEV)
    req_of = jax.vmap(lambda own, number: routed_block(jax.random.fold_in(splits[2], 2), own, number, TOK_DEV, REQS, 1, CAP, 2))(req_of_keys, req_of_turns).reshape((TOKENS, 1))
    cache = draw_cache(jax.random.fold_in(splits[5], 71), 0)
    cache_len = set_ends(jax.random.randint(splits[4], (REQS,), 2, CTX_LEN + 1), jax.random.fold_in(splits[4], 1), 2, CTX_LEN).astype(jnp.int32)
    return dict(queries=queries, q_pos=q_pos, req_of=req_of, cache=cache, cache_len=cache_len)


def reference(queries, q_pos, req_of, cache, cache_len):
    scale = HD ** -0.5
    width = 32
    blocks = queries.shape[0] // width

    def one_block(args):
        q_block, pos_block, req_block = args
        query = q_block.reshape(width, H, HD).astype(jnp.float32)
        length = cache_len[req_block]

        def one_shard(index):
            start = index * CTX_DEV
            span = lax.dynamic_slice_in_dim(cache, start, CTX_DEV, 1)[req_block]
            keys = span[:, :, :HD].astype(jnp.float32)
            values = span[:, :, HD:].astype(jnp.float32)
            key_pos = start + jnp.arange(CTX_DEV, dtype=jnp.int32)
            live = (key_pos[None, :] < length[:, None]) & (key_pos[None, :] <= pos_block[:, None])
            live3 = live[:, None, :]
            scores = jnp.einsum('thd,tkd->thk', query, keys) * scale
            scores = jnp.where(live3, scores, jnp.float32(-1e30))
            top = jnp.max(scores, axis=-1)
            weights = jnp.where(live3, jnp.exp(scores - top[..., None]), jnp.float32(0.0))
            total = jnp.sum(weights, axis=-1)
            rounded = lax.optimization_barrier(weights.astype(jnp.bfloat16)).astype(jnp.float32)
            safe = jnp.where(total > 0.0, total, jnp.float32(1.0))
            part = (jnp.einsum('thk,tkd->thd', rounded, values) / safe[..., None]).astype(jnp.bfloat16)
            lse = jnp.where(total > 0.0, top + jnp.log(safe), jnp.float32(-1e30))
            return part, lse

        parts, lses = lax.map(one_shard, jnp.arange(N_CTX, dtype=jnp.int32))
        parts = lax.optimization_barrier(parts).astype(jnp.float32)
        high = jnp.max(lses, axis=0)
        share = jnp.exp(lses - high[None])
        merged = jnp.sum(share[..., None] * parts, axis=0) / jnp.sum(share, axis=0)[..., None]
        return merged.reshape(width, H * HD).astype(jnp.bfloat16)

    result = lax.map(one_block, (queries.reshape(blocks, width, H * HD), q_pos.reshape(blocks, width), req_of[:, 0].reshape(blocks, width)))
    return result.reshape(queries.shape[0], H * HD)
```

```python
import functools
import math

import jax
import jax.numpy as jnp
from jax import lax
from jax.experimental import pallas as pl
from jax.experimental.pallas import tpu as pltpu
from jax.sharding import PartitionSpec as P

H = 16
HD = 128
WIDE = H * HD
META = 128
BALANCE = True
LOW = -1e30
SCALE = HD**-0.5
EXP_SCALE = SCALE * math.log2(math.e)
NT = (((1,), (1,)), ((), ()))
NN = (((1,), (0,)), ((), ()))
VMEM = pl.BlockSpec(memory_space=pltpu.VMEM)
SMEM = pl.BlockSpec(memory_space=pltpu.SMEM)


def dot(a, b, dims=NN):
    return lax.dot_general(a, b, dims, preferred_element_type=jnp.float32)


def iota(shape, dim):
    return lax.broadcasted_iota(jnp.int32, shape, dim)


def row_of(column):
    return jnp.transpose(jnp.broadcast_to(column, (column.shape[0], 128)), (1, 0))[:1, :]


def call(body, out_shape, in_specs, name, scratch=(), limit=32, cost=None):
    many = isinstance(out_shape, list)
    return pl.pallas_call(
        body,
        out_shape=out_shape,
        in_specs=in_specs,
        out_specs=[VMEM] * len(out_shape) if many else VMEM,
        scratch_shapes=list(scratch),
        compiler_params=pltpu.CompilerParams(vmem_limit_bytes=limit << 20),
        cost_estimate=cost,
        name=name,
    )


def route_kernel(block, me_ref, req_ref, pos_ref, q_ref, *outs):
    sends, back_ref = outs[:-1], outs[-1]
    rows = q_ref.shape[0]
    target_c = req_ref[...]
    target_r = row_of(target_c.astype(jnp.float32)).astype(jnp.int32)
    earlier_c = (target_c == target_r) & (iota((rows, rows), 1) < iota((rows, rows), 0))
    earlier_r = (target_c == target_r) & (iota((rows, rows), 0) < iota((rows, rows), 1))
    rank_c = jnp.sum(earlier_c.astype(jnp.int32), axis=1, keepdims=True)
    rank_r = jnp.sum(earlier_r.astype(jnp.int32), axis=0, keepdims=True)
    slot_c = (target_c ^ me_ref[1]) * block + rank_c
    slot_r = (target_r ^ me_ref[1]) * block + rank_r
    total = len(sends) * block
    back_ref[...] = (slot_c == iota((rows, total), 1)).astype(jnp.bfloat16)
    place = (slot_r == iota((total, rows), 0)).astype(jnp.bfloat16)
    plus = pos_ref[...] + 1
    place_f = place.astype(jnp.float32)
    high = jnp.sum(place_f * (plus >> 8).astype(jnp.float32), axis=1, keepdims=True)
    low = jnp.sum(place_f * (plus & 255).astype(jnp.float32), axis=1, keepdims=True)
    lane = iota((total, META), 1)
    meta = jnp.where(lane == 0, high, jnp.where(lane == 1, low, 0.0)).astype(jnp.bfloat16)
    moved = dot(place, q_ref[...]).astype(jnp.bfloat16)
    for d, out in enumerate(sends):
        out[:, :WIDE] = moved[d * block : (d + 1) * block]
        out[:, WIDE:] = meta[d * block : (d + 1) * block]


def sort_kernel(*refs):
    blocks, out, back_ref = refs[:-2], refs[-2], refs[-1]
    slots = out.shape[0]
    joined = jnp.concatenate([b[...] for b in blocks], axis=0)
    total = joined.shape[0]
    meta = joined[:, WIDE:].astype(jnp.float32)
    pos_c = meta[:, 0:1] * 256.0 + meta[:, 1:2]
    pos_r = row_of(pos_c)
    i0, i1 = iota((total, total), 0), iota((total, total), 1)
    ahead_r = (pos_c > pos_r) | ((pos_c == pos_r) & (i0 < i1))
    ahead_c = (pos_r > pos_c) | ((pos_r == pos_c) & (i1 < i0))
    rank_r = jnp.sum(ahead_r.astype(jnp.int32), axis=0, keepdims=True)
    rank_c = jnp.sum(ahead_c.astype(jnp.int32), axis=1, keepdims=True)
    place = (rank_r == iota((slots, total), 0)).astype(jnp.bfloat16)
    back_ref[...] = (rank_c == iota((total, slots), 1)).astype(jnp.bfloat16)
    out[...] = dot(place, joined).astype(jnp.bfloat16)


def keys_kernel(*refs):
    pieces, k_ref, vt_ref = refs[:-2], refs[-2], refs[-1]
    piece = pieces[0].shape[0]
    for i, ref in enumerate(pieces):
        k_ref[i * piece : (i + 1) * piece, :] = ref[:, :HD]
        vt_ref[:HD, i * piece : (i + 1) * piece] = jnp.transpose(ref[:, HD:], (1, 0))
    extra = vt_ref.shape[0] - HD
    ones = (iota((extra, vt_ref.shape[1]), 0) == 0).astype(jnp.bfloat16)
    vt_ref[HD:, :] = ones


def flash_kernel(pieces, piece, step, info_ref, len_ref, pq_ref, k_ref, vt_ref, out_ref, acc_ref, q_ref):
    length = len_ref[info_ref[2 * pieces]]
    slots = pq_ref.shape[0]

    def tile(first, count):
        width = count * H
        rows = pl.ds(first, count)
        meta = pq_ref[rows, WIDE:].astype(jnp.float32)
        pos = meta[:, 0:1] * 256.0 + meta[:, 1:2] - 1.0
        last = jnp.minimum(pos, (length - 1).astype(jnp.float32))
        top_last = jnp.max(last).astype(jnp.int32)
        last_r = jnp.concatenate([row_of(last)] * H, axis=1).astype(jnp.int32)
        live = jnp.int32(0)
        for b in range(pieces):
            live += (info_ref[b] <= top_last).astype(jnp.int32)
        for h in range(H):
            q_ref[h * count : (h + 1) * count, :] = pq_ref[rows, h * HD : (h + 1) * HD]
        acc_ref[:, :width] = jnp.zeros((acc_ref.shape[0], width), jnp.float32)

        def body(b, top):
            base = info_ref[pieces + b] * piece
            start = info_ref[b]

            def scores(g):
                keys = pl.ds(pl.multiple_of(base + g * step, step), step)
                return dot(k_ref[keys, :], q_ref[:width, :], NT)

            s = scores(0)
            for g in range(piece // step):
                later = scores(g + 1) if (g + 1) * step < piece else None
                s = jnp.where(iota((step, width), 0) <= last_r - (start + g * step), s, LOW)
                new = jnp.maximum(top, jnp.max(s, axis=0, keepdims=True))
                weights = jnp.exp2((s - new) * EXP_SCALE).astype(jnp.bfloat16)
                keys = pl.ds(pl.multiple_of(base + g * step, step), step)
                acc_ref[:, :width] = acc_ref[:, :width] * jnp.exp2((top - new) * EXP_SCALE) + dot(
                    vt_ref[:, keys], weights
                )
                top, s = new, later
            return top

        top = lax.fori_loop(0, live, body, jnp.full((1, width), 0.1 * LOW, jnp.float32))
        total = acc_ref[HD : HD + 1, :width]
        some = total > 0.0
        safe = jnp.where(some, total, 1.0)
        part = jnp.transpose(acc_ref[:HD, :width] / safe, (1, 0))
        lse = jnp.where(some, top * SCALE + jnp.log(safe), LOW)
        lse = jnp.transpose(jnp.broadcast_to(lse, (128, width)), (1, 0))
        lane = iota((count, META), 1)
        packed = jnp.zeros((count, META), jnp.float32)
        for h in range(H):
            out_ref[rows, h * HD : (h + 1) * HD] = part[h * count : (h + 1) * count].astype(jnp.bfloat16)
            packed = jnp.where(lane % H == h, lse[h * count : (h + 1) * count], packed)
        a = packed.astype(jnp.bfloat16).astype(jnp.float32)
        b = (packed - a).astype(jnp.bfloat16).astype(jnp.float32)
        c = packed - a - b
        packed = jnp.where(lane < H, a, jnp.where(lane < 2 * H, b, jnp.where(lane < 3 * H, c, 0.0)))
        out_ref[rows, WIDE:] = packed.astype(jnp.bfloat16)

    big = 32

    def one(j, carry):
        tile(pl.multiple_of(j * big, big), big)
        return carry

    lax.fori_loop(0, slots // big, one, 0)
    if slots % big:
        tile(slots // big * big, slots % big)


def merge_kernel(count, *refs):
    parts, back_ref, outs = refs[:count], refs[count], refs[count + 1 :]
    lses = []
    for part in parts:
        meta = part[:, WIDE:].astype(jnp.float32)
        lses.append(meta[:, :H] + meta[:, H : 2 * H] + meta[:, 2 * H : 3 * H])
    high = functools.reduce(jnp.maximum, lses)
    shares = [jnp.exp(lse - high) for lse in lses]
    total = functools.reduce(jnp.add, shares)
    shares = [share / total for share in shares]
    block = outs[0].shape[0]
    for h in range(H):
        cols = slice(h * HD, (h + 1) * HD)
        merged = sum(s[:, h : h + 1] * p[:, cols].astype(jnp.float32) for s, p in zip(shares, parts))
        placed = dot(back_ref[...], merged.astype(jnp.bfloat16)).astype(jnp.bfloat16)
        for d, out in enumerate(outs):
            out[:, cols] = placed[d * block : (d + 1) * block]


def unroute_kernel(*refs):
    blocks, back_ref, out = refs[:-2], refs[-2], refs[-1]
    joined = jnp.concatenate([b[...] for b in blocks], axis=0)
    out[...] = dot(back_ref[...], joined).astype(jnp.bfloat16)


def swapped(block, axis, distance):
    devices = range(lax.axis_size(axis))
    return lax.ppermute(block, axis, [(i, i ^ distance) for i in devices])


def per_device(queries, q_pos, req_of, cache, cache_len):
    tok_rows = queries.shape[0]
    groups = lax.axis_size("req")
    cycle = lax.axis_size("ctx")
    chips = cycle // 2
    capacity = 5 * tok_rows // (4 * groups)
    slots = groups * capacity
    block = -(-capacity // 8) * 8
    wide = WIDE + META
    shard_len = cache.shape[1]
    half = shard_len // 2
    here = lax.axis_index("ctx")
    mine = lax.axis_index("req")
    me = jnp.stack([here, mine]).astype(jnp.int32)
    bf = lambda *shape: jax.ShapeDtypeStruct(shape, jnp.bfloat16)

    *sends, back_tok = call(
        functools.partial(route_kernel, block),
        [bf(block, wide)] * groups + [bf(tok_rows, groups * block)],
        [SMEM] + [VMEM] * 3,
        "route",
    )(me, req_of, q_pos.reshape(1, tok_rows), queries)
    blocks = [sends[0]] + [swapped(sends[d], "req", d) for d in range(1, groups)]

    span = cache[0]
    other = cycle - 2
    kept, away = span[:half], span[half:]
    chip = here // 2
    if BALANCE:
        away = swapped(away, "ctx", other)
        partner = here ^ other
    else:
        partner = here
    kept_sib, away_sib = swapped(kept, "ctx", 1), swapped(away, "ctx", 1)
    pieces = [kept, kept_sib, away, away_sib]
    starts = jnp.stack(
        [here * shard_len, (here ^ 1) * shard_len, partner * shard_len + half, (partner ^ 1) * shard_len + half]
    ).astype(jnp.int32)
    order = jnp.sum(starts[None, :] < starts[:, None], axis=1)
    onehot = order[None, :] == jnp.arange(4)[:, None]
    info = jnp.concatenate(
        [
            jnp.sum(jnp.where(onehot, starts[None, :], 0), axis=1),
            jnp.sum(jnp.where(onehot, jnp.arange(4)[None, :], 0), axis=1),
            mine[None],
        ]
    ).astype(jnp.int32)
    keys = 4 * half
    k_all, vt_all = call(keys_kernel, [bf(keys, HD), bf(HD + 16, keys)], [VMEM] * 4, "keys")(*pieces)

    sorted_q, back_slot = call(
        sort_kernel, [bf(slots, wide), bf(groups * block, slots)], [VMEM] * groups, "sort"
    )(*blocks)
    visiting = [sorted_q] + [swapped(sorted_q, "ctx", 2 * d) for d in range(1, chips)]

    flash = call(
        functools.partial(flash_kernel, 4, half, 384),
        bf(slots, wide),
        [SMEM, SMEM] + [VMEM] * 3,
        "flash",
        scratch=[pltpu.VMEM((HD + 16, 512), jnp.float32), pltpu.VMEM((512, HD), jnp.bfloat16)],
        limit=48,
        cost=pl.CostEstimate(
            flops=4 * slots * H * keys * HD, bytes_accessed=keys * 512, transcendentals=slots * H * keys
        ),
    )
    parts = [flash(info, cache_len, q, k_all, vt_all) for q in visiting]
    home = [parts[0]] + [swapped(parts[d], "ctx", 2 * d) for d in range(1, chips)]
    outs = call(
        functools.partial(merge_kernel, chips), [bf(block, WIDE)] * groups, [VMEM] * (chips + 1), "merge"
    )(*home, back_slot)
    back = [outs[0]] + [swapped(outs[d], "req", d) for d in range(1, groups)]
    return call(unroute_kernel, bf(tok_rows, WIDE), [VMEM] * (groups + 1), "unroute")(*back, back_tok)


def solution(mesh):
    in_specs = (
        P(("ctx", "req"), None),
        P(("ctx", "req")),
        P(("ctx", "req"), None),
        P("req", "ctx", None),
        P(),
    )
    out_specs = P(("ctx", "req"), None)
    return jax.shard_map(
        per_device, mesh=mesh, in_specs=in_specs, out_specs=out_specs, check_vma=False
    )
```

```python
import functools
import math

import jax
import jax.numpy as jnp
from jax import lax
from jax.experimental import pallas as pl
from jax.experimental.pallas import tpu as pltpu
from jax.sharding import PartitionSpec as P

H = 16
HD = 128
WIDE = H * HD
META = 128
LOW = -1e30
SCALE = HD**-0.5
EXP_SCALE = SCALE * math.log2(math.e)
NT = (((1,), (1,)), ((), ()))
NN = (((1,), (0,)), ((), ()))
VMEM = pl.BlockSpec(memory_space=pltpu.VMEM)
SMEM = pl.BlockSpec(memory_space=pltpu.SMEM)


def dot(a, b, dims=NN):
    return lax.dot_general(a, b, dims, preferred_element_type=jnp.float32)


def iota(shape, dim):
    return lax.broadcasted_iota(jnp.int32, shape, dim)


def row_of(column):
    return jnp.transpose(jnp.broadcast_to(column, (column.shape[0], 128)), (1, 0))[:1, :]


def call(body, out_shape, in_specs, name, scratch=(), limit=32, cost=None, aliases=None):
    many = isinstance(out_shape, list)
    return pl.pallas_call(
        body,
        out_shape=out_shape,
        in_specs=in_specs,
        out_specs=[VMEM] * len(out_shape) if many else VMEM,
        scratch_shapes=list(scratch),
        compiler_params=pltpu.CompilerParams(vmem_limit_bytes=limit << 20),
        cost_estimate=cost,
        input_output_aliases=aliases or {},
        name=name,
    )


def route_kernel(block, me_ref, req_ref, pos_ref, q_ref, *outs):
    sends, back_ref = outs[:-1], outs[-1]
    rows = q_ref.shape[0]
    target_c = req_ref[...]
    target_r = row_of(target_c.astype(jnp.float32)).astype(jnp.int32)
    earlier_c = (target_c == target_r) & (iota((rows, rows), 1) < iota((rows, rows), 0))
    earlier_r = (target_c == target_r) & (iota((rows, rows), 0) < iota((rows, rows), 1))
    rank_c = jnp.sum(earlier_c.astype(jnp.int32), axis=1, keepdims=True)
    rank_r = jnp.sum(earlier_r.astype(jnp.int32), axis=0, keepdims=True)
    slot_c = (target_c ^ me_ref[1]) * block + rank_c
    slot_r = (target_r ^ me_ref[1]) * block + rank_r
    total = len(sends) * block
    back_ref[...] = (slot_c == iota((rows, total), 1)).astype(jnp.bfloat16)
    place = (slot_r == iota((total, rows), 0)).astype(jnp.bfloat16)
    plus = pos_ref[...] + 1
    place_f = place.astype(jnp.float32)
    high = jnp.sum(place_f * (plus >> 8).astype(jnp.float32), axis=1, keepdims=True)
    low = jnp.sum(place_f * (plus & 255).astype(jnp.float32), axis=1, keepdims=True)
    lane = iota((total, META), 1)
    meta = jnp.where(lane == 0, high, jnp.where(lane == 1, low, 0.0)).astype(jnp.bfloat16)
    moved = dot(place, q_ref[...]).astype(jnp.bfloat16)
    for d, out in enumerate(sends):
        out[:, :WIDE] = moved[d * block : (d + 1) * block]
        out[:, WIDE:] = meta[d * block : (d + 1) * block]


def sort_kernel(*refs):
    blocks, out, back_ref = refs[:-2], refs[-2], refs[-1]
    slots = out.shape[0]
    joined = jnp.concatenate([b[...] for b in blocks], axis=0)
    total = joined.shape[0]
    meta = joined[:, WIDE:].astype(jnp.float32)
    pos_c = meta[:, 0:1] * 256.0 + meta[:, 1:2]
    pos_r = row_of(pos_c)
    i0, i1 = iota((total, total), 0), iota((total, total), 1)
    ahead_r = (pos_c > pos_r) | ((pos_c == pos_r) & (i0 < i1))
    ahead_c = (pos_r > pos_c) | ((pos_r == pos_c) & (i1 < i0))
    rank_r = jnp.sum(ahead_r.astype(jnp.int32), axis=0, keepdims=True)
    rank_c = jnp.sum(ahead_c.astype(jnp.int32), axis=1, keepdims=True)
    place = (rank_r == iota((slots, total), 0)).astype(jnp.bfloat16)
    back_ref[...] = (rank_c == iota((total, slots), 1)).astype(jnp.bfloat16)
    out[...] = dot(place, joined).astype(jnp.bfloat16)


def keys_kernel(first, count, *refs):
    pieces, k_ref, vt_ref = refs[:count], refs[-2], refs[-1]
    piece = pieces[0].shape[0]
    extra = vt_ref.shape[0] - HD
    ones = (iota((extra, piece), 0) == 0).astype(jnp.bfloat16)
    for i, ref in enumerate(pieces, first):
        at = slice(i * piece, (i + 1) * piece)
        k_ref[at, :] = ref[:, :HD]
        vt_ref[:HD, at] = jnp.transpose(ref[:, HD:], (1, 0))
        vt_ref[HD:, at] = ones


def flash_kernel(pieces, piece, step, info_ref, len_ref, pq_ref, k_ref, vt_ref, out_ref, acc_ref, q_ref):
    length = len_ref[info_ref[2 * pieces]]
    slots = pq_ref.shape[0]

    def tile(first, count):
        width = count * H
        rows = pl.ds(first, count)
        meta = pq_ref[rows, WIDE:].astype(jnp.float32)
        pos = meta[:, 0:1] * 256.0 + meta[:, 1:2] - 1.0
        last = jnp.minimum(pos, (length - 1).astype(jnp.float32))
        top_last = jnp.max(last).astype(jnp.int32)
        last_r = jnp.concatenate([row_of(last)] * H, axis=1).astype(jnp.int32)
        live = jnp.int32(0)
        for b in range(pieces):
            live += (info_ref[b] <= top_last).astype(jnp.int32)
        for h in range(H):
            q_ref[h * count : (h + 1) * count, :] = pq_ref[rows, h * HD : (h + 1) * HD]
        acc_ref[:, :width] = jnp.zeros((acc_ref.shape[0], width), jnp.float32)

        def body(b, top):
            base = info_ref[pieces + b] * piece
            start = info_ref[b]

            def scores(g):
                keys = pl.ds(pl.multiple_of(base + g * step, step), step)
                return dot(k_ref[keys, :], q_ref[:width, :], NT)

            s = scores(0)
            for g in range(piece // step):
                later = scores(g + 1) if (g + 1) * step < piece else None
                s = jnp.where(iota((step, width), 0) <= last_r - (start + g * step), s, LOW)
                new = jnp.maximum(top, jnp.max(s, axis=0, keepdims=True))
                weights = jnp.exp2((s - new) * EXP_SCALE).astype(jnp.bfloat16)
                keys = pl.ds(pl.multiple_of(base + g * step, step), step)
                acc_ref[:, :width] = acc_ref[:, :width] * jnp.exp2((top - new) * EXP_SCALE) + dot(
                    vt_ref[:, keys], weights
                )
                top, s = new, later
            return top

        top = lax.fori_loop(0, live, body, jnp.full((1, width), 0.1 * LOW, jnp.float32))
        total = acc_ref[HD : HD + 1, :width]
        some = total > 0.0
        safe = jnp.where(some, total, 1.0)
        part = jnp.transpose(acc_ref[:HD, :width] / safe, (1, 0))
        lse = jnp.where(some, top * SCALE + jnp.log(safe), LOW)
        lse = jnp.transpose(jnp.broadcast_to(lse, (128, width)), (1, 0))
        lane = iota((count, META), 1)
        packed = jnp.zeros((count, META), jnp.float32)
        for h in range(H):
            out_ref[rows, h * HD : (h + 1) * HD] = part[h * count : (h + 1) * count].astype(jnp.bfloat16)
            packed = jnp.where(lane % H == h, lse[h * count : (h + 1) * count], packed)
        a = packed.astype(jnp.bfloat16).astype(jnp.float32)
        b = (packed - a).astype(jnp.bfloat16).astype(jnp.float32)
        c = packed - a - b
        packed = jnp.where(lane < H, a, jnp.where(lane < 2 * H, b, jnp.where(lane < 3 * H, c, 0.0)))
        out_ref[rows, WIDE:] = packed.astype(jnp.bfloat16)

    big = 32

    def one(j, carry):
        tile(pl.multiple_of(j * big, big), big)
        return carry

    lax.fori_loop(0, slots // big, one, 0)
    if slots % big:
        tile(slots // big * big, slots % big)


def merge_kernel(count, *refs):
    parts, back_ref, outs = refs[:count], refs[count], refs[count + 1 :]
    lses = []
    for part in parts:
        meta = part[:, WIDE:].astype(jnp.float32)
        lses.append(meta[:, :H] + meta[:, H : 2 * H] + meta[:, 2 * H : 3 * H])
    high = functools.reduce(jnp.maximum, lses)
    shares = [jnp.exp(lse - high) for lse in lses]
    total = functools.reduce(jnp.add, shares)
    shares = [share / total for share in shares]
    block = outs[0].shape[0]
    for h in range(H):
        cols = slice(h * HD, (h + 1) * HD)
        merged = sum(s[:, h : h + 1] * p[:, cols].astype(jnp.float32) for s, p in zip(shares, parts))
        placed = dot(back_ref[...], merged.astype(jnp.bfloat16)).astype(jnp.bfloat16)
        for d, out in enumerate(outs):
            out[:, cols] = placed[d * block : (d + 1) * block]


def unroute_kernel(*refs):
    blocks, back_ref, out = refs[:-2], refs[-2], refs[-1]
    joined = jnp.concatenate([b[...] for b in blocks], axis=0)
    out[...] = dot(back_ref[...], joined).astype(jnp.bfloat16)


def swapped(block, axis, distance):
    devices = range(lax.axis_size(axis))
    return lax.ppermute(block, axis, [(i, i ^ distance) for i in devices])


def per_device(queries, q_pos, req_of, cache, cache_len):
    tok_rows = queries.shape[0]
    groups = lax.axis_size("req")
    cycle = lax.axis_size("ctx")
    chips = cycle // 2
    capacity = 5 * tok_rows // (4 * groups)
    slots = groups * capacity
    block = -(-capacity // 8) * 8
    wide = WIDE + META
    shard_len = cache.shape[1]
    half = shard_len // 2
    here = lax.axis_index("ctx")
    mine = lax.axis_index("req")
    me = jnp.stack([here, mine]).astype(jnp.int32)
    bf = lambda *shape: jax.ShapeDtypeStruct(shape, jnp.bfloat16)

    span = cache[0]
    other = cycle - 2
    kept, away = span[:half], span[half:]
    away = swapped(away, "ctx", other)

    *sends, back_tok = call(
        functools.partial(route_kernel, block),
        [bf(block, wide)] * groups + [bf(tok_rows, groups * block)],
        [SMEM] + [VMEM] * 3,
        "route",
    )(me, req_of, q_pos.reshape(1, tok_rows), queries)
    blocks = [sends[0]] + [swapped(sends[d], "req", d) for d in range(1, groups)]
    kept, blocks[0] = lax.optimization_barrier((kept, blocks[0]))
    kept_sib = swapped(kept, "ctx", 1)
    all_keys = [bf(4 * half, HD), bf(HD + 16, 4 * half)]
    first = call(functools.partial(keys_kernel, 0, 2), all_keys, [VMEM] * 2, "keys_kept")(kept, kept_sib)

    sorted_q, back_slot = call(
        sort_kernel, [bf(slots, wide), bf(groups * block, slots)], [VMEM] * groups, "sort"
    )(*blocks)
    near = [swapped(sorted_q, "ctx", 2 * d) for d in range(1, chips) if d & (d - 1) == 0]
    mine_first, away = lax.optimization_barrier((sorted_q, away))

    def key_info(starts, first=0):
        count = len(starts)
        starts = jnp.stack(starts).astype(jnp.int32)
        order = jnp.sum(starts[None, :] < starts[:, None], axis=1)
        onehot = order[None, :] == jnp.arange(count)[:, None]
        return jnp.concatenate(
            [
                jnp.sum(jnp.where(onehot, starts[None, :], 0), axis=1),
                first + jnp.sum(jnp.where(onehot, jnp.arange(count)[None, :], 0), axis=1),
                mine[None],
            ]
        ).astype(jnp.int32)

    def flash(info, q, k, vt):
        pieces = info.shape[0] // 2
        keys = pieces * half
        return call(
            functools.partial(flash_kernel, pieces, half, 384),
            bf(slots, wide),
            [SMEM, SMEM] + [VMEM] * 3,
            "flash",
            scratch=[pltpu.VMEM((HD + 16, 512), jnp.float32), pltpu.VMEM((512, HD), jnp.bfloat16)],
            limit=48,
            cost=pl.CostEstimate(
                flops=4 * slots * H * keys * HD, bytes_accessed=keys * 512, transcendentals=slots * H * keys
            ),
        )(info, cache_len, q, k, vt)

    partner = here ^ other
    kept_at = [here * shard_len, (here ^ 1) * shard_len]
    away_at = [partner * shard_len + half, (partner ^ 1) * shard_len + half]
    own_kept = flash(key_info(kept_at), mine_first, *first)
    away_sib = swapped(away, "ctx", 1)
    own_kept, *first = lax.optimization_barrier((own_kept, *first))
    k_all, vt_all = call(
        functools.partial(keys_kernel, 2, 2), all_keys, [VMEM] * 4, "keys_away", aliases={2: 0, 3: 1}
    )(away, away_sib, *first)
    info = key_info(kept_at + away_at)
    far = [swapped(sorted_q, "ctx", 2 * d) for d in range(1, chips) if d & (d - 1) != 0]
    turn = own_kept
    parts = {}
    waiting = dict(zip([d for d in range(1, chips) if d & (d - 1) == 0], near))
    waiting.update(zip([d for d in range(1, chips) if d & (d - 1) != 0], far))
    for d in waiting:
        turn, q = lax.optimization_barrier((turn, waiting[d]))
        if d == 1:
            own_kept = turn
        else:
            parts[before] = turn
        turn = flash(info, q, k_all, vt_all)
        before = d
    parts[before] = turn
    home = [swapped(parts[d], "ctx", 2 * d) for d in parts]
    last, q = lax.optimization_barrier((turn, sorted_q))
    own_away = flash(key_info(away_at, 2), q, k_all, vt_all)
    home += [own_kept, own_away]
    outs = call(
        functools.partial(merge_kernel, chips + 1), [bf(block, WIDE)] * groups, [VMEM] * (chips + 2), "merge"
    )(*home, back_slot)
    back = [outs[0]] + [swapped(outs[d], "req", d) for d in range(1, groups)]
    return call(unroute_kernel, bf(tok_rows, WIDE), [VMEM] * (groups + 1), "unroute")(*back, back_tok)


def solution(mesh):
    in_specs = (
        P(("ctx", "req"), None),
        P(("ctx", "req")),
        P(("ctx", "req"), None),
        P("req", "ctx", None),
        P(),
    )
    out_specs = P(("ctx", "req"), None)
    return jax.shard_map(
        per_device, mesh=mesh, in_specs=in_specs, out_specs=out_specs, check_vma=False
    )
```

```python
import functools
import math

import jax
import jax.numpy as jnp
from jax import lax
from jax.experimental import pallas as pl
from jax.experimental.pallas import tpu as pltpu
from jax.sharding import PartitionSpec as P

H = 16
HD = 128
WIDE = H * HD
META = 128
LOW = -1e30
TILE = 32
PIECES = 4
OUT_ROWS = HD + 8
EXP_SCALE = HD**-0.5 * math.log2(math.e)
NT = (((1,), (1,)), ((), ()))
NN = (((1,), (0,)), ((), ()))
VMEM = pl.BlockSpec(memory_space=pltpu.VMEM)
SMEM = pl.BlockSpec(memory_space=pltpu.SMEM)


def dot(a, b, dims=NN):
    return lax.dot_general(a, b, dims, preferred_element_type=jnp.float32)


def iota(shape, dim):
    return lax.broadcasted_iota(jnp.int32, shape, dim)


def row_of(column):
    return jnp.transpose(jnp.broadcast_to(column, (column.shape[0], 128)), (1, 0))[:1, :]


def call(body, out_shape, in_specs, name, scratch=(), limit=48, aliases=None):
    many = isinstance(out_shape, list)
    return pl.pallas_call(
        body,
        out_shape=out_shape,
        in_specs=in_specs,
        out_specs=[VMEM] * len(out_shape) if many else VMEM,
        scratch_shapes=list(scratch),
        compiler_params=pltpu.CompilerParams(vmem_limit_bytes=limit << 20),
        cost_estimate=pl.CostEstimate(flops=1, bytes_accessed=1, transcendentals=0),
        input_output_aliases=aliases or {},
        name=name,
    )


def fold_of(capacity):
    fold = 1
    while capacity * fold % 8:
        fold *= 2
    return fold


def route_kernel(capacity, me_ref, req_ref, pos_ref, q_ref, *outs):
    sends, back_ref = outs[:-1], outs[-1]
    rows = q_ref.shape[0]
    fold = fold_of(capacity)
    block, width = capacity * fold, WIDE // fold
    target_c = req_ref[...]
    target_r = row_of(target_c.astype(jnp.float32)).astype(jnp.int32)
    same = target_c == target_r
    i0, i1 = iota((rows, rows), 0), iota((rows, rows), 1)
    rank_c = jnp.sum((same & (i1 < i0)).astype(jnp.int32), axis=1, keepdims=True)
    rank_r = jnp.sum((same & (i0 < i1)).astype(jnp.int32), axis=0, keepdims=True)
    slot_c = (target_c ^ me_ref[1]) * block + rank_c
    slot_r = (target_r ^ me_ref[1]) * block + rank_r
    total = len(sends) * block
    moved = jnp.zeros((total, width), jnp.float32)
    taken = jnp.zeros((total, rows), jnp.float32)
    for f in range(fold):
        back_ref[f] = (slot_c + f * capacity == iota((rows, total), 1)).astype(jnp.bfloat16)
        place = (slot_r + f * capacity == iota((total, rows), 0)).astype(jnp.float32)
        moved += dot(place.astype(jnp.bfloat16), q_ref[:, f * width : (f + 1) * width])
        taken += place
    plus = pos_ref[...] + 1
    high = jnp.sum(taken * (plus >> 8).astype(jnp.float32), axis=1, keepdims=True)
    low = jnp.sum(taken * (plus & 255).astype(jnp.float32), axis=1, keepdims=True)
    lane = iota((total, META), 1)
    meta = jnp.where(lane == 0, high, jnp.where(lane == 1, low, 0.0)).astype(jnp.bfloat16)
    moved = moved.astype(jnp.bfloat16)
    for d, out in enumerate(sends):
        out[:, :width] = moved[d * block : (d + 1) * block]
        out[:, width:] = meta[d * block : (d + 1) * block]


def row_parts(shape, dim, capacity):
    fold = fold_of(capacity)
    row = iota(shape, dim)
    token = jnp.zeros(shape, jnp.int32)
    part = jnp.zeros(shape, jnp.int32)
    for i in range(1, shape[dim] // capacity):
        passed = (row >= i * capacity).astype(jnp.int32)
        part += passed if i % fold else (1 - fold) * passed
    token = row - part * capacity
    for i in range(1, shape[dim] // (capacity * fold)):
        token -= (row >= i * capacity * fold).astype(jnp.int32) * (capacity * fold - capacity)
    return token, part


def sort_kernel(capacity, *refs):
    blocks, out, back_ref = refs[:-2], refs[-2], refs[-1]
    slots = out.shape[0]
    fold = fold_of(capacity)
    width = WIDE // fold
    joined = jnp.concatenate([b[...] for b in blocks], axis=0)
    total = joined.shape[0]
    meta = joined[:, width:].astype(jnp.float32)
    pos_c = meta[:, 0:1] * 256.0 + meta[:, 1:2]
    pos_r = row_of(pos_c)
    token_c, part_c = row_parts((total, 1), 0, capacity)
    token_r, part_r = row_parts((1, total), 1, capacity)
    ahead_r = ((pos_c > pos_r) | ((pos_c == pos_r) & (token_c < token_r))) & (part_c == 0)
    ahead_c = ((pos_r > pos_c) | ((pos_r == pos_c) & (token_r < token_c))) & (part_r == 0)
    rank_r = jnp.sum(ahead_r.astype(jnp.int32), axis=0, keepdims=True)
    rank_c = jnp.sum(ahead_c.astype(jnp.int32), axis=1, keepdims=True)
    place = rank_r == iota((slots, total), 0)
    for f in range(fold):
        mine = (place & (part_r == f)).astype(jnp.bfloat16)
        out[:, f * width : (f + 1) * width] = dot(mine, joined[:, :width]).astype(jnp.bfloat16)
        if f == 0:
            out[:, WIDE:] = dot(mine, joined[:, width:]).astype(jnp.bfloat16)
        back_ref[f] = ((rank_c == iota((total, slots), 1)) & (part_c == f)).astype(jnp.bfloat16)


def keys_kernel(me_ref, own_ref, sibling_ref, k_ref, vt_ref):
    shard = own_ref.shape[0]
    side = lax.rem(me_ref[0], 2)
    for ref, at in ((own_ref, side * shard), (sibling_ref, (1 - side) * shard)):
        rows = pl.ds(pl.multiple_of(at, 128), shard)
        k_ref[rows, :HD] = ref[:, :HD]
        k_ref[rows, HD:] = ref[:, :HD]
        vt_ref[:HD, rows] = jnp.transpose(ref[:, HD:], (1, 0))
    extra = vt_ref.shape[0] - HD
    vt_ref[HD:, :] = (iota((extra, 2 * shard), 0) == 0).astype(jnp.bfloat16)


def tiles_of(slots):
    return [(a, min(TILE, slots - a)) for a in range(0, slots, TILE)]


def flash_kernel(pieces, piece, info_ref, len_ref, pq_ref, k_ref, vt_ref, out_ref, q_ref, acc_ref, row_ref, s_ref, top_ref, live_ref):
    slots = pq_ref.shape[0]
    length = len_ref[info_ref[2 * pieces]]
    subs = [(0, 256), (256, piece - 256)]
    meta = pq_ref[:, WIDE:].astype(jnp.float32)
    pos = meta[:, 0:1] * 256.0 + meta[:, 1:2] - 1.0
    last = jnp.minimum(pos, (length - 1).astype(jnp.float32))
    for j, (a, count) in enumerate(tiles_of(slots)):
        here = last[a : a + count]
        top = jnp.max(here).astype(jnp.int32)
        live = jnp.int32(0)
        for i in range(pieces):
            live += (info_ref[i] <= top).astype(jnp.int32)
        live_ref[j] = live
        row_ref[0:1, a * H : (a + count) * H] = jnp.concatenate([row_of(here)] * H, axis=1)
        for h in range(H):
            x = pq_ref[a : a + count, h * HD : (h + 1) * HD].astype(jnp.float32) * EXP_SCALE
            high = x.astype(jnp.bfloat16)
            at = slice(a * H + h * count, a * H + (h + 1) * count)
            q_ref[at, :HD] = high
            q_ref[at, HD:] = (x - high.astype(jnp.float32)).astype(jnp.bfloat16)

    def tile(j, base, count):
        width = count * H
        cols = pl.ds(base, width)
        live = live_ref[j]

        @pl.when(live == 0)
        def _():
            out_ref[:, cols] = jnp.where(iota((OUT_ROWS, width), 0) == HD, LOW, 0.0).astype(jnp.bfloat16)

        @pl.when(live > 0)
        def _():
            def keys(c, a, n):
                return pl.ds(pl.multiple_of(info_ref[pieces + c] * piece + a, 128), n)

            def scores(c, a, n):
                return dot(k_ref[keys(c, a, n), :], q_ref[cols, :], NT)

            def masked(s, c, a):
                limit = row_ref[0:1, cols].astype(jnp.int32) - (info_ref[c] + a)
                return jnp.where(iota(s.shape, 0) <= limit, s, LOW)

            s_ref[:, :width] = scores(0, *subs[0])
            acc_ref[:, :width] = jnp.zeros((acc_ref.shape[0], width), jnp.float32)

            def pair(i, carry):
                steps = [(2 * i + k, a, n) for k in (0, 1) for a, n in subs]
                steps.append((jnp.minimum(2 * i + 2, pieces - 2), *subs[0]))
                s = s_ref[:, :width]
                total = None
                for (c, a, n), later in zip(steps, steps[1:]):
                    next_s = scores(*later)
                    weights = jnp.exp2(masked(s, c, a)).astype(jnp.bfloat16)
                    term = dot(vt_ref[:, keys(c, a, n)], weights)
                    total = term if total is None else total + term
                    s = next_s
                s_ref[:, :width] = s
                acc_ref[:, :width] += total
                return carry

            lax.fori_loop(0, (live + 1) // 2, pair, 0)
            top_ref[0:1, :width] = jnp.zeros((1, width), jnp.float32)
            total = acc_ref[HD : HD + 1, :width]
            dead = row_ref[0:1, cols] < info_ref[0].astype(jnp.float32)
            fine = dead | ((total > 2.0**-60) & (total < 2.0**100))

            @pl.when(jnp.logical_not(jnp.min(fine.astype(jnp.float32)) > 0.5))
            def _():
                acc_ref[:, :width] = jnp.zeros((acc_ref.shape[0], width), jnp.float32)
                top_ref[0:1, :width] = jnp.full((1, width), 0.1 * LOW, jnp.float32)

                def careful(i, carry):
                    c, a = i // (piece // 128), i % (piece // 128) * 128
                    s = masked(scores(c, a, 128), c, a)
                    before = top_ref[0:1, :width]
                    after = jnp.maximum(before, jnp.max(s, axis=0, keepdims=True))
                    weights = jnp.exp2(s - after).astype(jnp.bfloat16)
                    acc_ref[:, :width] = acc_ref[:, :width] * jnp.exp2(before - after) + dot(
                        vt_ref[:, keys(c, a, 128)], weights
                    )
                    top_ref[0:1, :width] = after
                    return carry

                lax.fori_loop(0, live * (piece // 128), careful, 0)

            total = acc_ref[HD : HD + 1, :width]
            some = total > 0.0
            safe = jnp.where(some, total, 1.0)
            out_ref[:HD, cols] = (acc_ref[:HD, :width] * (1.0 / safe)).astype(jnp.bfloat16)
            lse = jnp.where(some, top_ref[0:1, :width] + jnp.log2(safe), LOW)
            a = lse.astype(jnp.bfloat16).astype(jnp.float32)
            b = (lse - a).astype(jnp.bfloat16).astype(jnp.float32)
            row = iota((OUT_ROWS - HD, width), 0)
            terms = jnp.where(row == 0, a, jnp.where(row == 1, b, jnp.where(row == 2, lse - a - b, 0.0)))
            out_ref[HD:, cols] = terms.astype(jnp.bfloat16)

    whole = slots // TILE

    def one(j, carry):
        tile(j, pl.multiple_of(j * (TILE * H), TILE * H), TILE)
        return carry

    lax.fori_loop(0, whole, one, 0)
    if slots % TILE:
        tile(whole, whole * TILE * H, slots % TILE)


def merge_kernel(count, *refs):
    parts, back_ref, outs, slot_ref = refs[:count], refs[count], refs[count + 1 : -1], refs[-1]
    fold = back_ref.shape[0]
    slots = slot_ref.shape[0]
    for a, n in tiles_of(slots):
        cols = slice(a * H, (a + n) * H)
        lses = [sum(part[HD + i : HD + i + 1, cols].astype(jnp.float32) for i in range(3)) for part in parts]
        high = functools.reduce(jnp.maximum, lses)
        shares = [jnp.exp2(lse - high) for lse in lses]
        scale = 1.0 / functools.reduce(jnp.add, shares)
        merged = sum((share * scale) * part[:HD, cols].astype(jnp.float32) for share, part in zip(shares, parts))
        merged = jnp.transpose(merged, (1, 0)).astype(jnp.bfloat16)
        for h in range(H):
            slot_ref[a : a + n, h * HD : (h + 1) * HD] = merged[h * n : (h + 1) * n]
    block, width = outs[0].shape
    placed = sum(dot(back_ref[f], slot_ref[:, f * width : (f + 1) * width]) for f in range(fold))
    placed = placed.astype(jnp.bfloat16)
    for d, out in enumerate(outs):
        out[...] = placed[d * block : (d + 1) * block]


def unroute_kernel(*refs):
    blocks, back_ref, out = refs[:-2], refs[-2], refs[-1]
    width = blocks[0].shape[1]
    joined = jnp.concatenate([b[...] for b in blocks], axis=0)
    for f in range(back_ref.shape[0]):
        out[:, f * width : (f + 1) * width] = dot(back_ref[f], joined).astype(jnp.bfloat16)


def swapped(block, axis, distance):
    devices = range(lax.axis_size(axis))
    return lax.ppermute(block, axis, [(i, i ^ distance) for i in devices])


def per_device(queries, q_pos, req_of, cache, cache_len):
    tok_rows = queries.shape[0]
    groups = lax.axis_size("req")
    cycle = lax.axis_size("ctx")
    chips = cycle // 2
    capacity = 5 * tok_rows // (4 * groups)
    slots = groups * capacity
    fold = fold_of(capacity)
    block, width = capacity * fold, WIDE // fold
    shard_len = cache.shape[1]
    here = lax.axis_index("ctx")
    mine = lax.axis_index("req")
    me = jnp.stack([here, mine]).astype(jnp.int32)
    bf = lambda *shape: jax.ShapeDtypeStruct(shape, jnp.bfloat16)

    span = cache[0]
    sibling = swapped(span, "ctx", 1)

    *sends, back_tok = call(
        functools.partial(route_kernel, capacity),
        [bf(block, width + META)] * groups + [bf(fold, tok_rows, groups * block)],
        [SMEM] + [VMEM] * 3,
        "route",
    )(me, req_of, q_pos.reshape(1, tok_rows), queries)
    blocks = [sends[0]] + [swapped(sends[d], "req", d) for d in range(1, groups)]

    sorted_q, back_slot = call(
        functools.partial(sort_kernel, capacity),
        [bf(slots, WIDE + META), bf(fold, groups * block, slots)],
        [VMEM] * groups,
        "sort",
    )(*blocks)
    visiting = {d: swapped(sorted_q, "ctx", 2 * d) for d in range(1, chips)}
    sorted_q, span, sibling = lax.optimization_barrier((sorted_q, span, sibling))
    k_all, vt_all = call(
        keys_kernel, [bf(2 * shard_len, 2 * HD), bf(HD + 16, 2 * shard_len)], [SMEM] + [VMEM] * 2, "keys"
    )(me, span, sibling)
    info = jnp.concatenate(
        [
            here // 2 * (2 * shard_len) + jnp.arange(PIECES) * (2 * shard_len // PIECES),
            jnp.arange(PIECES),
            mine[None],
        ]
    ).astype(jnp.int32)

    def flash(q):
        widest = min(TILE, slots) * H
        return call(
            functools.partial(flash_kernel, PIECES, 2 * shard_len // PIECES),
            bf(OUT_ROWS, slots * H),
            [SMEM, SMEM] + [VMEM] * 3,
            "flash",
            scratch=[
                pltpu.VMEM((slots * H, 2 * HD), jnp.bfloat16),
                pltpu.VMEM((HD + 16, widest), jnp.float32),
                pltpu.VMEM((8, slots * H), jnp.float32),
                pltpu.VMEM((256, widest), jnp.float32),
                pltpu.VMEM((8, widest), jnp.float32),
                pltpu.SMEM((len(tiles_of(slots)),), jnp.int32),
            ],
        )(info, cache_len, q, k_all, vt_all)

    turn = flash(sorted_q)
    home = [turn]
    for d in sorted(visiting, key=lambda d: (d & (d - 1) != 0, d)):
        turn, q = lax.optimization_barrier((turn, visiting[d]))
        turn = flash(q)
        if d == chips - 1:
            turn, *home = lax.optimization_barrier((turn, *home))
        home.append(swapped(turn, "ctx", 2 * d))
    outs = call(
        functools.partial(merge_kernel, len(home)),
        [bf(block, width)] * groups,
        [VMEM] * (len(home) + 1),
        "merge",
        scratch=[pltpu.VMEM((slots, WIDE), jnp.bfloat16)],
    )(*home, back_slot)
    back = [outs[0]] + [swapped(outs[d], "req", d) for d in range(1, groups)]
    return call(unroute_kernel, bf(tok_rows, WIDE), [VMEM] * (groups + 1), "unroute")(*back, back_tok)


def solution(mesh):
    in_specs = (
        P(("ctx", "req"), None),
        P(("ctx", "req")),
        P(("ctx", "req"), None),
        P("req", "ctx", None),
        P(),
    )
    out_specs = P(("ctx", "req"), None)
    return jax.shard_map(
        per_device, mesh=mesh, in_specs=in_specs, out_specs=out_specs, check_vma=False
    )
```

```python
import functools
import math

import jax
import jax.numpy as jnp
from jax import lax
from jax.experimental import pallas as pl
from jax.experimental.pallas import tpu as pltpu
from jax.sharding import PartitionSpec as P

H = 16
HD = 128
WIDE = H * HD
META = 128
LOW = -1e30
TILE = 16
SUB = 256
OUT_ROWS = HD + 8
EXP_SCALE = HD**-0.5 * math.log2(math.e)
NT = (((1,), (1,)), ((), ()))
NN = (((1,), (0,)), ((), ()))
VMEM = pl.BlockSpec(memory_space=pltpu.VMEM)
SMEM = pl.BlockSpec(memory_space=pltpu.SMEM)


def dot(a, b, dims=NN):
    return lax.dot_general(a, b, dims, preferred_element_type=jnp.float32)


def iota(shape, dim):
    return lax.broadcasted_iota(jnp.int32, shape, dim)


def row_of(column):
    return jnp.transpose(jnp.broadcast_to(column, (column.shape[0], 128)), (1, 0))[:1, :]


def call(body, out_shape, in_specs, name, scratch=(), limit=48, aliases=None):
    many = isinstance(out_shape, list)
    return pl.pallas_call(
        body,
        out_shape=out_shape,
        in_specs=in_specs,
        out_specs=[VMEM] * len(out_shape) if many else VMEM,
        scratch_shapes=list(scratch),
        compiler_params=pltpu.CompilerParams(vmem_limit_bytes=limit << 20),
        cost_estimate=pl.CostEstimate(flops=1, bytes_accessed=1, transcendentals=0),
        input_output_aliases=aliases or {},
        name=name,
    )


def fold_of(capacity):
    fold = 1
    while capacity * fold % 8:
        fold *= 2
    return fold


def route_kernel(capacity, me_ref, req_ref, pos_ref, q_ref, *outs):
    sends, back_ref = outs[:-1], outs[-1]
    rows = q_ref.shape[0]
    fold = fold_of(capacity)
    block, width = capacity * fold, WIDE // fold
    target_c = req_ref[...]
    target_r = row_of(target_c.astype(jnp.float32)).astype(jnp.int32)
    same = target_c == target_r
    i0, i1 = iota((rows, rows), 0), iota((rows, rows), 1)
    rank_c = jnp.sum((same & (i1 < i0)).astype(jnp.int32), axis=1, keepdims=True)
    rank_r = jnp.sum((same & (i0 < i1)).astype(jnp.int32), axis=0, keepdims=True)
    slot_c = (target_c ^ me_ref[1]) * block + rank_c
    slot_r = (target_r ^ me_ref[1]) * block + rank_r
    total = len(sends) * block
    moved = jnp.zeros((total, width), jnp.float32)
    taken = jnp.zeros((total, rows), jnp.float32)
    for f in range(fold):
        back_ref[f] = (slot_c + f * capacity == iota((rows, total), 1)).astype(jnp.bfloat16)
        place = (slot_r + f * capacity == iota((total, rows), 0)).astype(jnp.float32)
        moved += dot(place.astype(jnp.bfloat16), q_ref[:, f * width : (f + 1) * width])
        taken += place
    plus = pos_ref[...] + 1
    high = jnp.sum(taken * (plus >> 8).astype(jnp.float32), axis=1, keepdims=True)
    low = jnp.sum(taken * (plus & 255).astype(jnp.float32), axis=1, keepdims=True)
    lane = iota((total, META), 1)
    meta = jnp.where(lane == 0, high, jnp.where(lane == 1, low, 0.0)).astype(jnp.bfloat16)
    moved = moved.astype(jnp.bfloat16)
    for d, out in enumerate(sends):
        out[:, :width] = moved[d * block : (d + 1) * block]
        out[:, width:] = meta[d * block : (d + 1) * block]


def row_parts(shape, dim, capacity):
    fold = fold_of(capacity)
    row = iota(shape, dim)
    token = jnp.zeros(shape, jnp.int32)
    part = jnp.zeros(shape, jnp.int32)
    for i in range(1, shape[dim] // capacity):
        passed = (row >= i * capacity).astype(jnp.int32)
        part += passed if i % fold else (1 - fold) * passed
    token = row - part * capacity
    for i in range(1, shape[dim] // (capacity * fold)):
        token -= (row >= i * capacity * fold).astype(jnp.int32) * (capacity * fold - capacity)
    return token, part


def sort_kernel(capacity, *refs):
    blocks, out, back_ref = refs[:-2], refs[-2], refs[-1]
    slots = out.shape[0]
    fold = fold_of(capacity)
    width = WIDE // fold
    joined = jnp.concatenate([b[...] for b in blocks], axis=0)
    total = joined.shape[0]
    meta = joined[:, width:].astype(jnp.float32)
    pos_c = meta[:, 0:1] * 256.0 + meta[:, 1:2]
    pos_r = row_of(pos_c)
    token_c, part_c = row_parts((total, 1), 0, capacity)
    token_r, part_r = row_parts((1, total), 1, capacity)
    ahead_r = ((pos_c > pos_r) | ((pos_c == pos_r) & (token_c < token_r))) & (part_c == 0)
    ahead_c = ((pos_r > pos_c) | ((pos_r == pos_c) & (token_r < token_c))) & (part_r == 0)
    rank_r = jnp.sum(ahead_r.astype(jnp.int32), axis=0, keepdims=True)
    rank_c = jnp.sum(ahead_c.astype(jnp.int32), axis=1, keepdims=True)
    place = rank_r == iota((slots, total), 0)
    for f in range(fold):
        mine = (place & (part_r == f)).astype(jnp.bfloat16)
        out[:, f * width : (f + 1) * width] = dot(mine, joined[:, :width]).astype(jnp.bfloat16)
        if f == 0:
            out[:, WIDE:] = dot(mine, joined[:, width:]).astype(jnp.bfloat16)
        back_ref[f] = ((rank_c == iota((total, slots), 1)) & (part_c == f)).astype(jnp.bfloat16)


def keys_kernel(first, count, *refs):
    pieces, k_ref, vt_ref = refs[:count], refs[-2], refs[-1]
    piece = pieces[0].shape[0]
    extra = vt_ref.shape[0] - HD
    ones = (iota((extra, piece), 0) == 0).astype(jnp.bfloat16)
    for i, ref in enumerate(pieces, first):
        at = slice(i * piece, (i + 1) * piece)
        k_ref[at, :HD] = ref[:, :HD]
        k_ref[at, HD:] = ref[:, :HD]
        vt_ref[:HD, at] = jnp.transpose(ref[:, HD:], (1, 0))
        vt_ref[HD:, at] = ones


def flash_kernel(
    first, chips, piece, me_ref, len_ref, pq_ref, k_ref, vt_ref, out_ref, q_ref, acc_ref, row_ref, s_ref, top_ref, job_ref, info_ref
):
    width = TILE * H
    all_width = out_ref.shape[1]
    tiles = all_width // width
    pieces, pairs = 4, 2
    length = len_ref[me_ref[1]]
    chip, core = me_ref[0] // 2, lax.rem(me_ref[0], 2)
    kept_at, away_at = chip * (4 * piece), (chips - 1 - chip) * (4 * piece) + piece
    rising = kept_at < away_at
    for pair, kept in enumerate((rising, jnp.logical_not(rising))):
        for k in range(2):
            info_ref[2 * pair + k] = jnp.where(kept, kept_at, away_at) + 2 * piece * k
            info_ref[pieces + 2 * pair + k] = jnp.where(kept, 0, 2) + jnp.where(core == k, 0, 1)
    meta = pq_ref[first * TILE : (first + tiles) * TILE, WIDE:].astype(jnp.float32)
    pos = meta[:, 0:1] * 256.0 + meta[:, 1:2] - 1.0
    last = jnp.minimum(pos, (length - 1).astype(jnp.float32))
    count = jnp.int32(0)
    for j in range(tiles):
        here = last[j * TILE : (j + 1) * TILE]
        top = jnp.max(here).astype(jnp.int32)
        for i in range(pairs):
            job_ref[count] = j * pairs + i
            count += (info_ref[2 * i] <= top).astype(jnp.int32)
        row_ref[0:1, j * width : (j + 1) * width] = jnp.concatenate([row_of(here)] * H, axis=1)
        rows = slice((first + j) * TILE, (first + j + 1) * TILE)
        for h in range(H):
            x = pq_ref[rows, h * HD : (h + 1) * HD].astype(jnp.float32) * EXP_SCALE
            high = x.astype(jnp.bfloat16)
            at = slice(j * width + h * TILE, j * width + (h + 1) * TILE)
            q_ref[at, :HD] = high
            q_ref[at, HD:] = (x - high.astype(jnp.float32)).astype(jnp.bfloat16)
    for k in range(3):
        job_ref[count + k] = tiles * pairs
    row_ref[0:1, all_width:] = jnp.full((1, width), -1.0, jnp.float32)
    q_ref[all_width:, :] = jnp.zeros((width, 2 * HD), jnp.bfloat16)
    acc_ref[...] = jnp.zeros_like(acc_ref)

    def place(job):
        tile = job // pairs
        return pl.ds(pl.multiple_of(tile * width, width), width), 2 * (job - tile * pairs)

    def keys(c, a, n):
        return pl.ds(pl.multiple_of(info_ref[pieces + c] * piece + a, 128), n)

    def scores(cols, c, a, n):
        return dot(k_ref[keys(c, a, n), :], q_ref[cols, :], NT)

    def masked(s, cols, c, a):
        limit = row_ref[0:1, cols].astype(jnp.int32) - (info_ref[c] + a)
        return jnp.where(iota(s.shape, 0) <= limit, s, LOW)

    subs = [(0, SUB), (SUB, piece - SUB)]

    @pl.when(count > 0)
    def _():
        for k in range(2):
            cols, c = place(job_ref[k])
            s_ref[k] = scores(cols, c, *subs[0])

    def turn(b, carry):
        now = [place(job_ref[2 * b + k]) for k in range(2)]
        later = [place(job_ref[2 * b + 2 + k]) for k in range(2)]
        steps = [(g, a, n) for g in range(2) for a, n in subs]
        s = [s_ref[k] for k in range(2)]
        totals = [None, None]
        for i, (g, a, n) in enumerate(steps):
            if i + 1 < len(steps):
                g2, a2, n2 = steps[i + 1]
                next_s = [scores(cols, c + g2, a2, n2) for cols, c in now]
            else:
                next_s = [scores(cols, c, *subs[0]) for cols, c in later]
            for k, (cols, c) in enumerate(now):
                weights = jnp.exp2(masked(s[k], cols, c + g, a)).astype(jnp.bfloat16)
                term = dot(vt_ref[:, keys(c + g, a, n)], weights)
                totals[k] = term if totals[k] is None else totals[k] + term
            s = next_s
        for k in range(2):
            s_ref[k] = s[k]
        for k, (cols, _) in enumerate(now):
            acc_ref[:, cols] += totals[k]
        return carry

    lax.fori_loop(0, (count + 1) // 2, turn, 0)
    top_ref[0:1, :] = jnp.zeros((1, all_width), jnp.float32)
    total = acc_ref[HD : HD + 1, :all_width]
    dead = row_ref[0:1, :all_width] < info_ref[0].astype(jnp.float32)
    fine = dead | ((total > 2.0**-60) & (total < 2.0**100))

    @pl.when(jnp.logical_not(jnp.min(fine.astype(jnp.float32)) > 0.5))
    def _():
        acc_ref[...] = jnp.zeros_like(acc_ref)
        top_ref[0:1, :] = jnp.full((1, all_width), 0.1 * LOW, jnp.float32)

        def careful(i, carry):
            chunks = piece // 128
            cols = pl.ds(pl.multiple_of(i // (pieces * chunks) * width, width), width)
            c, a = i % (pieces * chunks) // chunks, i % chunks * 128
            s = masked(scores(cols, c, a, 128), cols, c, a)
            before = top_ref[0:1, cols]
            after = jnp.maximum(before, jnp.max(s, axis=0, keepdims=True))
            weights = jnp.exp2(s - after).astype(jnp.bfloat16)
            acc_ref[:, cols] = acc_ref[:, cols] * jnp.exp2(before - after) + dot(vt_ref[:, keys(c, a, 128)], weights)
            top_ref[0:1, cols] = after
            return carry

        lax.fori_loop(0, tiles * pieces * (piece // 128), careful, 0)

    total = acc_ref[HD : HD + 1, :all_width]
    some = total > 0.0
    safe = jnp.where(some, total, 1.0)
    out_ref[:HD, :] = (acc_ref[:HD, :all_width] * (1.0 / safe)).astype(jnp.bfloat16)
    lse = jnp.where(some, top_ref[0:1, :] + jnp.log2(safe), LOW)
    a = lse.astype(jnp.bfloat16).astype(jnp.float32)
    b = (lse - a).astype(jnp.bfloat16).astype(jnp.float32)
    row = iota((OUT_ROWS - HD, all_width), 0)
    terms = jnp.where(row == 0, a, jnp.where(row == 1, b, jnp.where(row == 2, lse - a - b, 0.0)))
    out_ref[HD:, :] = terms.astype(jnp.bfloat16)


def merge_kernel(count, *refs):
    own, parts, back_ref, outs, slot_ref = refs[:2], refs[2 : count + 2], refs[count + 2], refs[count + 3 : -1], refs[-1]
    fold = back_ref.shape[0]
    width = TILE * H
    split = own[0].shape[1] // width
    for j in range(slot_ref.shape[0] // TILE):
        here = [(own[0], j) if j < split else (own[1], j - split)] + [(part, j) for part in parts]
        here = [(part, slice(i * width, (i + 1) * width)) for part, i in here]
        lses = [sum(part[HD + i : HD + i + 1, cols].astype(jnp.float32) for i in range(3)) for part, cols in here]
        high = functools.reduce(jnp.maximum, lses)
        shares = [jnp.exp2(lse - high) for lse in lses]
        scale = 1.0 / functools.reduce(jnp.add, shares)
        merged = sum((share * scale) * part[:HD, cols].astype(jnp.float32) for share, (part, cols) in zip(shares, here))
        merged = jnp.transpose(merged, (1, 0)).astype(jnp.bfloat16)
        for h in range(H):
            slot_ref[j * TILE : (j + 1) * TILE, h * HD : (h + 1) * HD] = merged[h * TILE : (h + 1) * TILE]
    block, cut = outs[0].shape
    placed = sum(dot(back_ref[f], slot_ref[:, f * cut : (f + 1) * cut]) for f in range(fold))
    placed = placed.astype(jnp.bfloat16)
    for d, out in enumerate(outs):
        out[...] = placed[d * block : (d + 1) * block]


def unroute_kernel(*refs):
    blocks, back_ref, out = refs[:-2], refs[-2], refs[-1]
    width = blocks[0].shape[1]
    joined = jnp.concatenate([b[...] for b in blocks], axis=0)
    for f in range(back_ref.shape[0]):
        out[:, f * width : (f + 1) * width] = dot(back_ref[f], joined).astype(jnp.bfloat16)


def swapped(block, axis, distance):
    devices = range(lax.axis_size(axis))
    return lax.ppermute(block, axis, [(i, i ^ distance) for i in devices])


def per_device(queries, q_pos, req_of, cache, cache_len):
    tok_rows = queries.shape[0]
    groups = lax.axis_size("req")
    cycle = lax.axis_size("ctx")
    chips = cycle // 2
    capacity = 5 * tok_rows // (4 * groups)
    slots = groups * capacity
    fold = fold_of(capacity)
    block, width = capacity * fold, WIDE // fold
    shard_len = cache.shape[1]
    half = shard_len // 2
    here = lax.axis_index("ctx")
    mine = lax.axis_index("req")
    me = jnp.stack([here, mine]).astype(jnp.int32)
    bf = lambda *shape: jax.ShapeDtypeStruct(shape, jnp.bfloat16)

    other = cycle - 2
    away = swapped(cache[0, half:], "ctx", other)

    *sends, back_tok = call(
        functools.partial(route_kernel, capacity),
        [bf(block, width + META)] * groups + [bf(fold, tok_rows, groups * block)],
        [SMEM] + [VMEM] * 3,
        "route",
    )(me, req_of, q_pos.reshape(1, tok_rows), queries)
    sends[0], kept = lax.optimization_barrier((sends[0], cache[0, :half]))
    blocks = [sends[0]] + [swapped(sends[d], "req", d) for d in range(1, groups)]
    kept_sib = swapped(kept, "ctx", 1)
    all_keys = [bf(4 * half, 2 * HD), bf(HD + 16, 4 * half)]
    kept_keys = call(functools.partial(keys_kernel, 0, 2), all_keys, [VMEM] * 2, "keys_kept")(kept, kept_sib)
    blocks[0], *kept_keys = lax.optimization_barrier((blocks[0], *kept_keys))

    sorted_q, back_slot = call(
        functools.partial(sort_kernel, capacity),
        [bf(slots, WIDE + META), bf(fold, groups * block, slots)],
        [VMEM] * groups,
        "sort",
    )(*blocks)
    visiting = {d: swapped(sorted_q, "ctx", 2 * d) for d in range(1, chips)}
    sorted_q, away = lax.optimization_barrier((sorted_q, away))
    away_sib = swapped(away, "ctx", 1)
    k_all, vt_all = call(
        functools.partial(keys_kernel, 2, 2), all_keys, [VMEM] * 4, "keys_away", aliases={2: 0, 3: 1}
    )(away, away_sib, *kept_keys)

    def flash(q, first=0, tiles=slots // TILE):
        extra = (tiles + 1) * TILE * H
        return call(
            functools.partial(flash_kernel, first, chips, half),
            bf(OUT_ROWS, tiles * TILE * H),
            [SMEM, SMEM] + [VMEM] * 3,
            "flash",
            scratch=[
                pltpu.VMEM((extra, 2 * HD), jnp.bfloat16),
                pltpu.VMEM((HD + 16, extra), jnp.float32),
                pltpu.VMEM((8, extra), jnp.float32),
                pltpu.VMEM((2, SUB, TILE * H), jnp.float32),
                pltpu.VMEM((8, tiles * TILE * H), jnp.float32),
                pltpu.SMEM((2 * tiles + 4,), jnp.int32),
                pltpu.SMEM((8,), jnp.int32),
            ],
        )(me, cache_len, q, k_all, vt_all)

    turn = flash(sorted_q, 0, 1)
    own = [turn]
    home = []
    for d in sorted(visiting, key=lambda d: (d & (d - 1) != 0, d)):
        turn, q = lax.optimization_barrier((turn, visiting[d]))
        turn = flash(q)
        if d == chips - 1:
            turn, *home = lax.optimization_barrier((turn, *home))
        home.append(swapped(turn, "ctx", 2 * d))
    turn, q = lax.optimization_barrier((turn, sorted_q))
    own.append(flash(q, 1, slots // TILE - 1))
    home = [*own, *home]
    outs = call(
        functools.partial(merge_kernel, len(home) - 2),
        [bf(block, width)] * groups,
        [VMEM] * (len(home) + 1),
        "merge",
        scratch=[pltpu.VMEM((slots, WIDE), jnp.bfloat16)],
    )(*home, back_slot)
    back = [outs[0]] + [swapped(outs[d], "req", d) for d in range(1, groups)]
    return call(unroute_kernel, bf(tok_rows, WIDE), [VMEM] * (groups + 1), "unroute")(*back, back_tok)


def solution(mesh):
    in_specs = (
        P(("ctx", "req"), None),
        P(("ctx", "req")),
        P(("ctx", "req"), None),
        P("req", "ctx", None),
        P(),
    )
    out_specs = P(("ctx", "req"), None)
    return jax.shard_map(
        per_device, mesh=mesh, in_specs=in_specs, out_specs=out_specs, check_vma=False
    )
```

```python
import functools
import math

import jax
import jax.numpy as jnp
from jax import lax
from jax.experimental import pallas as pl
from jax.experimental.pallas import tpu as pltpu
from jax.sharding import PartitionSpec as P

H = 16
HD = 128
WIDE = H * HD
META = 128
LOW = -1e30
TILE = 16
SUB = 256
OUT_ROWS = HD + 8
EXP_SCALE = HD**-0.5 * math.log2(math.e)
NT = (((1,), (1,)), ((), ()))
NN = (((1,), (0,)), ((), ()))
VMEM = pl.BlockSpec(memory_space=pltpu.VMEM)
SMEM = pl.BlockSpec(memory_space=pltpu.SMEM)


def dot(a, b, dims=NN):
    return lax.dot_general(a, b, dims, preferred_element_type=jnp.float32)


def in_hbm(x):
    return pltpu.with_memory_space_constraint(x, pltpu.HBM)


def iota(shape, dim):
    return lax.broadcasted_iota(jnp.int32, shape, dim)


def row_of(column):
    return jnp.transpose(jnp.broadcast_to(column, (column.shape[0], 128)), (1, 0))[:1, :]


def call(body, out_shape, in_specs, name, scratch=(), limit=20, aliases=None):
    many = isinstance(out_shape, list)
    return pl.pallas_call(
        body,
        out_shape=out_shape,
        in_specs=in_specs,
        out_specs=[VMEM] * len(out_shape) if many else VMEM,
        scratch_shapes=list(scratch),
        compiler_params=pltpu.CompilerParams(vmem_limit_bytes=limit << 20),
        cost_estimate=pl.CostEstimate(flops=1, bytes_accessed=1, transcendentals=0),
        input_output_aliases=aliases or {},
        name=name,
    )


def fold_of(capacity):
    fold = 1
    while capacity * fold % 8:
        fold *= 2
    return fold


def route_kernel(capacity, me_ref, req_hbm, pos_hbm, q_hbm, *outs):
    outs, (req_ref, pos_ref, q_ref, sem) = outs[:-4], outs[-4:]
    sends, back_ref = outs[:-1], outs[-1]
    fetches = [
        pltpu.make_async_copy(src, dst, sem.at[i])
        for i, (src, dst) in enumerate(((req_hbm, req_ref), (pos_hbm, pos_ref), (q_hbm, q_ref)))
    ]
    for fetch in fetches:
        fetch.start()
    for fetch in fetches:
        fetch.wait()
    rows = q_ref.shape[0]
    fold = fold_of(capacity)
    block, width = capacity * fold, WIDE // fold
    i0, i1 = iota((rows, rows), 0), iota((rows, rows), 1)
    target_r = req_ref[...]
    target_c = jnp.sum(jnp.where(i0 == i1, target_r, 0), axis=1, keepdims=True)
    same = target_c == target_r
    rank_c = jnp.sum((same & (i1 < i0)).astype(jnp.int32), axis=1, keepdims=True)
    rank_r = jnp.sum((same & (i0 < i1)).astype(jnp.int32), axis=0, keepdims=True)
    slot_c = (target_c ^ me_ref[1]) * block + rank_c
    slot_r = (target_r ^ me_ref[1]) * block + rank_r
    total = len(sends) * block
    moved = jnp.zeros((total, width), jnp.float32)
    taken = jnp.zeros((total, rows), jnp.float32)
    for f in range(fold):
        back_ref[f] = (slot_c + f * capacity == iota((rows, total), 1)).astype(jnp.bfloat16)
        place = (slot_r + f * capacity == iota((total, rows), 0)).astype(jnp.float32)
        moved += dot(place.astype(jnp.bfloat16), q_ref[:, f * width : (f + 1) * width])
        taken += place
    plus = pos_ref[...] + 1
    high = jnp.sum(taken * (plus >> 8).astype(jnp.float32), axis=1, keepdims=True)
    low = jnp.sum(taken * (plus & 255).astype(jnp.float32), axis=1, keepdims=True)
    lane = iota((total, META), 1)
    meta = jnp.where(lane == 0, high, jnp.where(lane == 1, low, 0.0)).astype(jnp.bfloat16)
    moved = moved.astype(jnp.bfloat16)
    for d, out in enumerate(sends):
        out[:, :width] = moved[d * block : (d + 1) * block]
        out[:, width:] = meta[d * block : (d + 1) * block]


def row_parts(shape, dim, capacity):
    fold = fold_of(capacity)
    row = iota(shape, dim)
    token = jnp.zeros(shape, jnp.int32)
    part = jnp.zeros(shape, jnp.int32)
    for i in range(1, shape[dim] // capacity):
        passed = (row >= i * capacity).astype(jnp.int32)
        part += passed if i % fold else (1 - fold) * passed
    token = row - part * capacity
    for i in range(1, shape[dim] // (capacity * fold)):
        token -= (row >= i * capacity * fold).astype(jnp.int32) * (capacity * fold - capacity)
    return token, part


def sort_kernel(capacity, *refs):
    blocks, out, back_ref = refs[:-2], refs[-2], refs[-1]
    slots = out.shape[0]
    fold = fold_of(capacity)
    width = WIDE // fold
    joined = jnp.concatenate([b[...] for b in blocks], axis=0)
    total = joined.shape[0]
    meta = joined[:, width:].astype(jnp.float32)
    pos_c = meta[:, 0:1] * 256.0 + meta[:, 1:2]
    pos_r = row_of(pos_c)
    token_c, part_c = row_parts((total, 1), 0, capacity)
    token_r, part_r = row_parts((1, total), 1, capacity)
    ahead_r = ((pos_c > pos_r) | ((pos_c == pos_r) & (token_c < token_r))) & (part_c == 0)
    ahead_c = ((pos_r > pos_c) | ((pos_r == pos_c) & (token_r < token_c))) & (part_r == 0)
    rank_r = jnp.sum(ahead_r.astype(jnp.int32), axis=0, keepdims=True)
    rank_c = jnp.sum(ahead_c.astype(jnp.int32), axis=1, keepdims=True)
    place = rank_r == iota((slots, total), 0)
    for f in range(fold):
        mine = (place & (part_r == f)).astype(jnp.bfloat16)
        out[:, f * width : (f + 1) * width] = dot(mine, joined[:, :width]).astype(jnp.bfloat16)
        if f == 0:
            out[:, WIDE:] = dot(mine, joined[:, width:]).astype(jnp.bfloat16)
        back_ref[f] = ((rank_c == iota((total, slots), 1)) & (part_c == f)).astype(jnp.bfloat16)


def store_keys(k_ref, vt_ref, number, piece):
    count = piece.shape[0]
    at = slice(number * count, (number + 1) * count)
    k_ref[at, :HD] = piece[:, :HD]
    k_ref[at, HD:] = piece[:, :HD]
    vt_ref[:HD, at] = jnp.transpose(piece[:, HD:], (1, 0))
    vt_ref[HD:, at] = (iota((vt_ref.shape[0] - HD, count), 0) == 0).astype(jnp.bfloat16)


def keys_kernel(first, pieces, *refs):
    k_ref, vt_ref = refs[-2:]
    at = 0
    for number, count in enumerate(pieces, first):
        store_keys(k_ref, vt_ref, number, jnp.concatenate([ref[...] for ref in refs[at : at + count]], axis=0))
        at += count


def flash_kernel(
    first, chips, piece, me_ref, len_ref, pq_ref, k_ref, vt_ref, out_ref, q_ref, acc_ref, row_ref, s_ref, top_ref, job_ref, info_ref
):
    width = TILE * H
    all_width = out_ref.shape[1]
    tiles = all_width // width
    pieces, pairs = 4, 2
    length = len_ref[me_ref[1]]
    chip, core = me_ref[0] // 2, lax.rem(me_ref[0], 2)
    home_at = chip * (4 * piece)
    away_at = (chips - 1 - chip) * (4 * piece) + piece
    rising = home_at < away_at
    for pair, kept in enumerate((rising, jnp.logical_not(rising))):
        for k in range(2):
            info_ref[2 * pair + k] = jnp.where(kept, home_at, away_at) + 2 * piece * k
            info_ref[pieces + 2 * pair + k] = jnp.where(kept, 0, 2) + jnp.where(core == k, 0, 1)
    meta = pq_ref[first * TILE : (first + tiles) * TILE, WIDE:].astype(jnp.float32)
    pos = meta[:, 0:1] * 256.0 + meta[:, 1:2] - 1.0
    last = jnp.minimum(pos, (length - 1).astype(jnp.float32))
    count = jnp.int32(0)
    for j in range(tiles):
        here = last[j * TILE : (j + 1) * TILE]
        top = jnp.max(here).astype(jnp.int32)
        for i in range(pairs):
            job_ref[count] = j * pairs + i
            count += (info_ref[2 * i] <= top).astype(jnp.int32)
        row_ref[0:1, j * width : (j + 1) * width] = jnp.concatenate([row_of(here)] * H, axis=1)
        rows = slice((first + j) * TILE, (first + j + 1) * TILE)
        for h in range(H):
            x = pq_ref[rows, h * HD : (h + 1) * HD].astype(jnp.float32) * EXP_SCALE
            high = x.astype(jnp.bfloat16)
            at = slice(j * width + h * TILE, j * width + (h + 1) * TILE)
            q_ref[at, :HD] = high
            q_ref[at, HD:] = (x - high.astype(jnp.float32)).astype(jnp.bfloat16)
    for k in range(3):
        job_ref[count + k] = tiles * pairs
    row_ref[0:1, all_width:] = jnp.full((1, width), -1.0, jnp.float32)
    q_ref[all_width:, :] = jnp.zeros((width, 2 * HD), jnp.bfloat16)
    acc_ref[...] = jnp.zeros_like(acc_ref)

    def place(job):
        tile = job // pairs
        return pl.ds(pl.multiple_of(tile * width, width), width), 2 * (job - tile * pairs)

    def keys(c, a, n):
        return pl.ds(pl.multiple_of(info_ref[pieces + c] * piece + a, 128), n)

    def scores(cols, c, a, n):
        return dot(k_ref[keys(c, a, n), :], q_ref[cols, :], NT)

    def masked(s, cols, c, a):
        limit = row_ref[0:1, cols].astype(jnp.int32) - (info_ref[c] + a)
        return jnp.where(iota(s.shape, 0) <= limit, s, LOW)

    subs = [(0, SUB), (SUB, piece - SUB)]

    @pl.when(count > 0)
    def _():
        for k in range(2):
            cols, c = place(job_ref[k])
            s_ref[k] = scores(cols, c, *subs[0])

    def turn(b, carry):
        now = [place(job_ref[2 * b + k]) for k in range(2)]
        later = [place(job_ref[2 * b + 2 + k]) for k in range(2)]
        steps = [(g, a, n) for g in range(2) for a, n in subs]
        s = [s_ref[k] for k in range(2)]
        totals = [None, None]
        for i, (g, a, n) in enumerate(steps):
            if i + 1 < len(steps):
                g2, a2, n2 = steps[i + 1]
                next_s = [scores(cols, c + g2, a2, n2) for cols, c in now]
            else:
                next_s = [scores(cols, c, *subs[0]) for cols, c in later]
            for k, (cols, c) in enumerate(now):
                weights = jnp.exp2(masked(s[k], cols, c + g, a)).astype(jnp.bfloat16)
                term = dot(vt_ref[:, keys(c + g, a, n)], weights)
                totals[k] = term if totals[k] is None else totals[k] + term
            s = next_s
        for k in range(2):
            s_ref[k] = s[k]
        for k, (cols, _) in enumerate(now):
            acc_ref[:, cols] += totals[k]
        return carry

    lax.fori_loop(0, (count + 1) // 2, turn, 0)
    top_ref[0:1, :] = jnp.zeros((1, all_width), jnp.float32)
    total = acc_ref[HD : HD + 1, :all_width]
    dead = row_ref[0:1, :all_width] < info_ref[0].astype(jnp.float32)
    fine = dead | ((total > 2.0**-60) & (total < 2.0**100))

    @pl.when(jnp.logical_not(jnp.min(fine.astype(jnp.float32)) > 0.5))
    def _():
        acc_ref[...] = jnp.zeros_like(acc_ref)
        top_ref[0:1, :] = jnp.full((1, all_width), 0.1 * LOW, jnp.float32)

        def careful(i, carry):
            chunks = piece // 128
            cols = pl.ds(pl.multiple_of(i // (pieces * chunks) * width, width), width)
            c, a = i % (pieces * chunks) // chunks, i % chunks * 128
            s = masked(scores(cols, c, a, 128), cols, c, a)
            before = top_ref[0:1, cols]
            after = jnp.maximum(before, jnp.max(s, axis=0, keepdims=True))
            weights = jnp.exp2(s - after).astype(jnp.bfloat16)
            acc_ref[:, cols] = acc_ref[:, cols] * jnp.exp2(before - after) + dot(vt_ref[:, keys(c, a, 128)], weights)
            top_ref[0:1, cols] = after
            return carry

        lax.fori_loop(0, tiles * pieces * (piece // 128), careful, 0)

    total = acc_ref[HD : HD + 1, :all_width]
    some = total > 0.0
    safe = jnp.where(some, total, 1.0)
    out_ref[:HD, :] = (acc_ref[:HD, :all_width] * (1.0 / safe)).astype(jnp.bfloat16)
    lse = jnp.where(some, top_ref[0:1, :] + jnp.log2(safe), LOW)
    a = lse.astype(jnp.bfloat16).astype(jnp.float32)
    b = (lse - a).astype(jnp.bfloat16).astype(jnp.float32)
    row = iota((OUT_ROWS - HD, all_width), 0)
    terms = jnp.where(row == 0, a, jnp.where(row == 1, b, jnp.where(row == 2, lse - a - b, 0.0)))
    out_ref[HD:, :] = terms.astype(jnp.bfloat16)


def merge_kernel(count, *refs):
    own, parts, back_ref, outs, slot_ref = refs[:2], refs[2 : count + 2], refs[count + 2], refs[count + 3 : -1], refs[-1]
    fold = back_ref.shape[0]
    width = TILE * H
    split = own[0].shape[1] // width
    for j in range(slot_ref.shape[0] // TILE):
        here = [(own[0], j) if j < split else (own[1], j - split)] + [(part, j) for part in parts]
        here = [(part, slice(i * width, (i + 1) * width)) for part, i in here]
        lses = [sum(part[HD + i : HD + i + 1, cols].astype(jnp.float32) for i in range(3)) for part, cols in here]
        high = functools.reduce(jnp.maximum, lses)
        shares = [jnp.exp2(lse - high) for lse in lses]
        scale = 1.0 / functools.reduce(jnp.add, shares)
        merged = sum((share * scale) * part[:HD, cols].astype(jnp.float32) for share, (part, cols) in zip(shares, here))
        merged = jnp.transpose(merged, (1, 0)).astype(jnp.bfloat16)
        for h in range(H):
            slot_ref[j * TILE : (j + 1) * TILE, h * HD : (h + 1) * HD] = merged[h * TILE : (h + 1) * TILE]
    block, cut = outs[0].shape
    placed = sum(dot(back_ref[f], slot_ref[:, f * cut : (f + 1) * cut]) for f in range(fold))
    placed = placed.astype(jnp.bfloat16)
    for d, out in enumerate(outs):
        out[...] = placed[d * block : (d + 1) * block]


def unroute_kernel(*refs):
    blocks, back_ref, out = refs[:-2], refs[-2], refs[-1]
    width = blocks[0].shape[1]
    joined = jnp.concatenate([b[...] for b in blocks], axis=0)
    for f in range(back_ref.shape[0]):
        out[:, f * width : (f + 1) * width] = dot(back_ref[f], joined).astype(jnp.bfloat16)


def swapped(block, axis, distance):
    devices = range(lax.axis_size(axis))
    return lax.ppermute(block, axis, [(i, i ^ distance) for i in devices])


def per_device(queries, q_pos, req_of, cache, cache_len):
    tok_rows = queries.shape[0]
    groups = lax.axis_size("req")
    cycle = lax.axis_size("ctx")
    chips = cycle // 2
    capacity = 5 * tok_rows // (4 * groups)
    slots = groups * capacity
    fold = fold_of(capacity)
    block, width = capacity * fold, WIDE // fold
    shard_len = cache.shape[1]
    half = shard_len // 2
    here = lax.axis_index("ctx")
    mine = lax.axis_index("req")
    me = jnp.stack([here, mine]).astype(jnp.int32)
    bf = lambda *shape: jax.ShapeDtypeStruct(shape, jnp.bfloat16)

    away = swapped(cache[0, half:], "ctx", cycle - 2)

    *sends, back_tok = call(
        functools.partial(route_kernel, capacity),
        [bf(block, width + META)] * groups + [bf(fold, tok_rows, groups * block)],
        [SMEM] + [pl.BlockSpec(memory_space=pltpu.HBM)] * 3,
        "route",
        scratch=[
            pltpu.VMEM((1, tok_rows), jnp.int32),
            pltpu.VMEM((1, tok_rows), jnp.int32),
            pltpu.VMEM((tok_rows, WIDE), jnp.bfloat16),
            pltpu.SemaphoreType.DMA((3,)),
        ],
    )(me, *[in_hbm(x) for x in (req_of.reshape(1, tok_rows), q_pos.reshape(1, tok_rows), queries)])
    blocks = {d: swapped(sends[d], "req", d) for d in reversed(range(1, groups))}
    blocks[0], span = lax.optimization_barrier((sends[0], cache[0]))
    kept = span[:half]
    kept_sib = swapped(kept, "ctx", 1)
    all_keys = [bf(4 * half, 2 * HD), bf(HD + 16, 4 * half)]
    kept_keys = call(functools.partial(keys_kernel, 0, (1, 1)), all_keys, [VMEM] * 2, "kept_keys")(kept, kept_sib)
    blocks[0], *kept_keys = lax.optimization_barrier((blocks[0], *kept_keys))

    sorted_q, back_slot = call(
        functools.partial(sort_kernel, capacity),
        [bf(slots, WIDE + META), bf(fold, groups * block, slots)],
        [VMEM] * groups,
        "sort",
    )(*[blocks[d] for d in range(groups)])
    visiting = {d: swapped(sorted_q, "ctx", 2 * d) for d in range(1, chips)}
    sorted_q, away = lax.optimization_barrier((sorted_q, away))
    away_sib = [swapped(away[i * half // 2 : (i + 1) * half // 2], "ctx", 1) for i in range(2)]

    k_all, vt_all = call(
        functools.partial(keys_kernel, 2, (1, 2)), all_keys, [VMEM] * 5, "away_keys", aliases={3: 0, 4: 1}
    )(away, *away_sib, *kept_keys)

    def flash(q, first=0, tiles=slots // TILE):
        extra = (tiles + 1) * TILE * H
        return call(
            functools.partial(flash_kernel, first, chips, half),
            bf(OUT_ROWS, tiles * TILE * H),
            [SMEM, SMEM] + [VMEM] * 3,
            "flash",
            scratch=[
                pltpu.VMEM((extra, 2 * HD), jnp.bfloat16),
                pltpu.VMEM((HD + 16, extra), jnp.float32),
                pltpu.VMEM((8, extra), jnp.float32),
                pltpu.VMEM((2, SUB, TILE * H), jnp.float32),
                pltpu.VMEM((8, tiles * TILE * H), jnp.float32),
                pltpu.SMEM((2 * tiles + 4,), jnp.int32),
                pltpu.SMEM((8,), jnp.int32),
            ],
        )(me, cache_len, q, k_all, vt_all)

    turn = flash(sorted_q, 0, 2)
    own = [turn]
    home = []
    for d in sorted(visiting, key=lambda d: (d & (d - 1) != 0, d)):
        turn, q = lax.optimization_barrier((turn, visiting[d]))
        turn = flash(q)
        if d == chips - 1:
            turn, *home = lax.optimization_barrier((turn, *home))
        home.append(swapped(turn, "ctx", 2 * d))
    turn, q = lax.optimization_barrier((turn, sorted_q))
    own.append(flash(q, 2, slots // TILE - 2))
    home = [*own, *home]
    outs = call(
        functools.partial(merge_kernel, len(home) - 2),
        [bf(block, width)] * groups,
        [VMEM] * (len(home) + 1),
        "merge",
        scratch=[pltpu.VMEM((slots, WIDE), jnp.bfloat16)],
    )(*home, back_slot)
    back = [outs[0]] + [swapped(outs[d], "req", d) for d in range(1, groups)]
    return call(unroute_kernel, bf(tok_rows, WIDE), [VMEM] * (groups + 1), "unroute")(*back, back_tok)


def solution(mesh):
    in_specs = (
        P(("ctx", "req"), None),
        P(("ctx", "req")),
        P(("ctx", "req"), None),
        P("req", "ctx", None),
        P(),
    )
    out_specs = P(("ctx", "req"), None)
    return jax.shard_map(
        per_device, mesh=mesh, in_specs=in_specs, out_specs=out_specs, check_vma=False
    )
```

```python
import functools
import math

import jax
import jax.numpy as jnp
from jax import lax
from jax.experimental import pallas as pl
from jax.experimental.pallas import tpu as pltpu
from jax.sharding import PartitionSpec as P

H = 16
HD = 128
WIDE = H * HD
META = 128
LOW = -1e30
TILE = 16
SUB = 256
OUT_ROWS = HD + 8
EXP_SCALE = HD**-0.5 * math.log2(math.e)
NT = (((1,), (1,)), ((), ()))
NN = (((1,), (0,)), ((), ()))
VMEM = pl.BlockSpec(memory_space=pltpu.VMEM)
SMEM = pl.BlockSpec(memory_space=pltpu.SMEM)


def dot(a, b, dims=NN):
    return lax.dot_general(a, b, dims, preferred_element_type=jnp.float32)


def in_hbm(x):
    return pltpu.with_memory_space_constraint(x, pltpu.HBM)


def iota(shape, dim):
    return lax.broadcasted_iota(jnp.int32, shape, dim)


def row_of(column):
    return jnp.transpose(jnp.broadcast_to(column, (column.shape[0], 128)), (1, 0))[:1, :]


def call(body, out_shape, in_specs, name, scratch=(), limit=20, aliases=None):
    many = isinstance(out_shape, list)
    return pl.pallas_call(
        body,
        out_shape=out_shape,
        in_specs=in_specs,
        out_specs=[VMEM] * len(out_shape) if many else VMEM,
        scratch_shapes=list(scratch),
        compiler_params=pltpu.CompilerParams(vmem_limit_bytes=limit << 20),
        cost_estimate=pl.CostEstimate(flops=1, bytes_accessed=1, transcendentals=0),
        input_output_aliases=aliases or {},
        name=name,
    )


def fold_of(capacity):
    fold = 1
    while capacity * fold % 8:
        fold *= 2
    return fold


def route_kernel(capacity, me_ref, req_hbm, pos_hbm, q_hbm, shard_hbm, *outs):
    outs, (req_ref, pos_ref, q_ref, sem) = outs[:-4], outs[-4:]
    sends, back_ref, halves = outs[:-3], outs[-3], outs[-2:]
    half = halves[0].shape[0]
    moves = [(req_hbm, req_ref), (pos_hbm, pos_ref), (q_hbm, q_ref)]
    moves += [(shard_hbm.at[pl.ds(i * half, half)], halves[i]) for i in range(2)]
    fetches = [pltpu.make_async_copy(src, dst, sem.at[i]) for i, (src, dst) in enumerate(moves)]
    for fetch in fetches:
        fetch.start()
    for fetch in fetches[:3]:
        fetch.wait()
    rows = q_ref.shape[0]
    fold = fold_of(capacity)
    block, width = capacity * fold, WIDE // fold
    i0, i1 = iota((rows, rows), 0), iota((rows, rows), 1)
    target_r = req_ref[...]
    target_c = jnp.sum(jnp.where(i0 == i1, target_r, 0), axis=1, keepdims=True)
    same = target_c == target_r
    rank_c = jnp.sum((same & (i1 < i0)).astype(jnp.int32), axis=1, keepdims=True)
    rank_r = jnp.sum((same & (i0 < i1)).astype(jnp.int32), axis=0, keepdims=True)
    slot_c = (target_c ^ me_ref[1]) * block + rank_c
    slot_r = (target_r ^ me_ref[1]) * block + rank_r
    total = len(sends) * block
    moved = jnp.zeros((total, width), jnp.float32)
    taken = jnp.zeros((total, rows), jnp.float32)
    for f in range(fold):
        back_ref[f] = (slot_c + f * capacity == iota((rows, total), 1)).astype(jnp.bfloat16)
        place = (slot_r + f * capacity == iota((total, rows), 0)).astype(jnp.float32)
        moved += dot(place.astype(jnp.bfloat16), q_ref[:, f * width : (f + 1) * width])
        taken += place
    plus = pos_ref[...] + 1
    high = jnp.sum(taken * (plus >> 8).astype(jnp.float32), axis=1, keepdims=True)
    low = jnp.sum(taken * (plus & 255).astype(jnp.float32), axis=1, keepdims=True)
    lane = iota((total, META), 1)
    meta = jnp.where(lane == 0, high, jnp.where(lane == 1, low, 0.0)).astype(jnp.bfloat16)
    moved = moved.astype(jnp.bfloat16)
    for d, out in enumerate(sends):
        out[:, :width] = moved[d * block : (d + 1) * block]
        out[:, width:] = meta[d * block : (d + 1) * block]
    for fetch in fetches[3:]:
        fetch.wait()


def row_parts(shape, dim, capacity):
    fold = fold_of(capacity)
    row = iota(shape, dim)
    token = jnp.zeros(shape, jnp.int32)
    part = jnp.zeros(shape, jnp.int32)
    for i in range(1, shape[dim] // capacity):
        passed = (row >= i * capacity).astype(jnp.int32)
        part += passed if i % fold else (1 - fold) * passed
    token = row - part * capacity
    for i in range(1, shape[dim] // (capacity * fold)):
        token -= (row >= i * capacity * fold).astype(jnp.int32) * (capacity * fold - capacity)
    return token, part


def sort_kernel(capacity, *refs):
    blocks, out, back_ref = refs[:-2], refs[-2], refs[-1]
    slots = out.shape[0]
    fold = fold_of(capacity)
    width = WIDE // fold
    joined = jnp.concatenate([b[...] for b in reversed(blocks)], axis=0)
    total = joined.shape[0]
    meta = joined[:, width:].astype(jnp.float32)
    pos_c = meta[:, 0:1] * 256.0 + meta[:, 1:2]
    pos_r = row_of(pos_c)
    token_c, part_c = row_parts((total, 1), 0, capacity)
    token_r, part_r = row_parts((1, total), 1, capacity)
    ahead_r = ((pos_c > pos_r) | ((pos_c == pos_r) & (token_c < token_r))) & (part_c == 0)
    ahead_c = ((pos_r > pos_c) | ((pos_r == pos_c) & (token_r < token_c))) & (part_r == 0)
    rank_r = jnp.sum(ahead_r.astype(jnp.int32), axis=0, keepdims=True)
    rank_c = jnp.sum(ahead_c.astype(jnp.int32), axis=1, keepdims=True)
    place = rank_r == iota((slots, total), 0)
    for f in range(fold):
        mine = (place & (part_r == f)).astype(jnp.bfloat16)
        out[:, f * width : (f + 1) * width] = dot(mine, joined[:, :width]).astype(jnp.bfloat16)
        if f == 0:
            out[:, WIDE:] = dot(mine, joined[:, width:]).astype(jnp.bfloat16)
        back_ref[f] = ((rank_c == iota((total, slots), 1)) & (part_c == f)).astype(jnp.bfloat16)


def store_keys(k_ref, vt_ref, number, piece):
    count = piece.shape[0]
    at = slice(number * count, (number + 1) * count)
    k_ref[at, :HD] = piece[:, :HD]
    k_ref[at, HD:] = piece[:, :HD]
    vt_ref[:HD, at] = jnp.transpose(piece[:, HD:], (1, 0))
    vt_ref[HD:, at] = (iota((vt_ref.shape[0] - HD, count), 0) == 0).astype(jnp.bfloat16)


def keys_kernel(first, pieces, *refs):
    k_ref, vt_ref = refs[-2:]
    at = 0
    for number, count in enumerate(pieces, first):
        store_keys(k_ref, vt_ref, number, jnp.concatenate([ref[...] for ref in refs[at : at + count]], axis=0))
        at += count


def flash_kernel(
    first, chips, piece, me_ref, len_ref, pq_ref, k_ref, vt_ref, out_ref, q_ref, acc_ref, row_ref, s_ref, top_ref, job_ref, info_ref
):
    width = TILE * H
    all_width = out_ref.shape[1]
    tiles = all_width // width
    pieces, pairs = 4, 2
    length = len_ref[me_ref[1]]
    chip, core = me_ref[0] // 2, lax.rem(me_ref[0], 2)
    home_at = chip * (4 * piece)
    away_at = (chips - 1 - chip) * (4 * piece) + piece
    rising = home_at < away_at
    for pair, kept in enumerate((rising, jnp.logical_not(rising))):
        for k in range(2):
            info_ref[2 * pair + k] = jnp.where(kept, home_at, away_at) + 2 * piece * k
            info_ref[pieces + 2 * pair + k] = jnp.where(kept, 0, 2) + jnp.where(core == k, 0, 1)
    meta = pq_ref[first * TILE : (first + tiles) * TILE, WIDE:].astype(jnp.float32)
    pos = meta[:, 0:1] * 256.0 + meta[:, 1:2] - 1.0
    last = jnp.minimum(pos, (length - 1).astype(jnp.float32))
    count = jnp.int32(0)
    for j in range(tiles):
        here = last[j * TILE : (j + 1) * TILE]
        top = jnp.max(here).astype(jnp.int32)
        for i in range(pairs):
            job_ref[count] = j * pairs + i
            count += (info_ref[2 * i] <= top).astype(jnp.int32)
        row_ref[0:1, j * width : (j + 1) * width] = jnp.concatenate([row_of(here)] * H, axis=1)
        rows = slice((first + j) * TILE, (first + j + 1) * TILE)
        for h in range(H):
            x = pq_ref[rows, h * HD : (h + 1) * HD].astype(jnp.float32) * EXP_SCALE
            high = x.astype(jnp.bfloat16)
            at = slice(j * width + h * TILE, j * width + (h + 1) * TILE)
            q_ref[at, :HD] = high
            q_ref[at, HD:] = (x - high.astype(jnp.float32)).astype(jnp.bfloat16)
    for k in range(3):
        job_ref[count + k] = tiles * pairs
    row_ref[0:1, all_width:] = jnp.full((1, width), -1.0, jnp.float32)
    q_ref[all_width:, :] = jnp.zeros((width, 2 * HD), jnp.bfloat16)
    acc_ref[...] = jnp.zeros_like(acc_ref)

    def place(job):
        tile = job // pairs
        return pl.ds(pl.multiple_of(tile * width, width), width), 2 * (job - tile * pairs)

    def keys(c, a, n):
        return pl.ds(pl.multiple_of(info_ref[pieces + c] * piece + a, 128), n)

    def scores(cols, c, a, n):
        return dot(k_ref[keys(c, a, n), :], q_ref[cols, :], NT)

    def masked(s, cols, c, a):
        limit = row_ref[0:1, cols].astype(jnp.int32) - (info_ref[c] + a)
        return jnp.where(iota(s.shape, 0) <= limit, s, LOW)

    subs = [(0, SUB), (SUB, piece - SUB)]

    @pl.when(count > 0)
    def _():
        for k in range(2):
            cols, c = place(job_ref[k])
            s_ref[k] = scores(cols, c, *subs[0])

    def turn(b, carry):
        now = [place(job_ref[2 * b + k]) for k in range(2)]
        later = [place(job_ref[2 * b + 2 + k]) for k in range(2)]
        steps = [(g, a, n) for g in range(2) for a, n in subs]
        s = [s_ref[k] for k in range(2)]
        totals = [None, None]
        for i, (g, a, n) in enumerate(steps):
            if i + 1 < len(steps):
                g2, a2, n2 = steps[i + 1]
                next_s = [scores(cols, c + g2, a2, n2) for cols, c in now]
            else:
                next_s = [scores(cols, c, *subs[0]) for cols, c in later]
            for k, (cols, c) in enumerate(now):
                weights = jnp.exp2(masked(s[k], cols, c + g, a)).astype(jnp.bfloat16)
                term = dot(vt_ref[:, keys(c + g, a, n)], weights)
                totals[k] = term if totals[k] is None else totals[k] + term
            s = next_s
        for k in range(2):
            s_ref[k] = s[k]
        for k, (cols, _) in enumerate(now):
            acc_ref[:, cols] += totals[k]
        return carry

    lax.fori_loop(0, (count + 1) // 2, turn, 0)
    top_ref[0:1, :] = jnp.zeros((1, all_width), jnp.float32)
    total = acc_ref[HD : HD + 1, :all_width]
    dead = row_ref[0:1, :all_width] < info_ref[0].astype(jnp.float32)
    fine = dead | ((total > 2.0**-60) & (total < 2.0**100))

    @pl.when(jnp.logical_not(jnp.min(fine.astype(jnp.float32)) > 0.5))
    def _():
        acc_ref[...] = jnp.zeros_like(acc_ref)
        top_ref[0:1, :] = jnp.full((1, all_width), 0.1 * LOW, jnp.float32)

        def careful(i, carry):
            chunks = piece // 128
            cols = pl.ds(pl.multiple_of(i // (pieces * chunks) * width, width), width)
            c, a = i % (pieces * chunks) // chunks, i % chunks * 128
            s = masked(scores(cols, c, a, 128), cols, c, a)
            before = top_ref[0:1, cols]
            after = jnp.maximum(before, jnp.max(s, axis=0, keepdims=True))
            weights = jnp.exp2(s - after).astype(jnp.bfloat16)
            acc_ref[:, cols] = acc_ref[:, cols] * jnp.exp2(before - after) + dot(vt_ref[:, keys(c, a, 128)], weights)
            top_ref[0:1, cols] = after
            return carry

        lax.fori_loop(0, tiles * pieces * (piece // 128), careful, 0)

    total = acc_ref[HD : HD + 1, :all_width]
    some = total > 0.0
    safe = jnp.where(some, total, 1.0)
    out_ref[:HD, :] = (acc_ref[:HD, :all_width] * (1.0 / safe)).astype(jnp.bfloat16)
    lse = jnp.where(some, top_ref[0:1, :] + jnp.log2(safe), LOW)
    a = lse.astype(jnp.bfloat16).astype(jnp.float32)
    b = (lse - a).astype(jnp.bfloat16).astype(jnp.float32)
    row = iota((OUT_ROWS - HD, all_width), 0)
    terms = jnp.where(row == 0, a, jnp.where(row == 1, b, jnp.where(row == 2, lse - a - b, 0.0)))
    out_ref[HD:, :] = terms.astype(jnp.bfloat16)


def merge_kernel(count, *refs):
    own, parts, back_ref, outs, slot_ref = refs[:2], refs[2 : count + 2], refs[count + 2], refs[count + 3 : -1], refs[-1]
    fold = back_ref.shape[0]
    width = TILE * H
    split = own[0].shape[1] // width
    for j in range(slot_ref.shape[0] // TILE):
        here = [(own[0], j) if j < split else (own[1], j - split)] + [(part, j) for part in parts]
        here = [(part, slice(i * width, (i + 1) * width)) for part, i in here]
        lses = [sum(part[HD + i : HD + i + 1, cols].astype(jnp.float32) for i in range(3)) for part, cols in here]
        high = functools.reduce(jnp.maximum, lses)
        shares = [jnp.exp2(lse - high) for lse in lses]
        scale = 1.0 / functools.reduce(jnp.add, shares)
        merged = sum((share * scale) * part[:HD, cols].astype(jnp.float32) for share, (part, cols) in zip(shares, here))
        merged = jnp.transpose(merged, (1, 0)).astype(jnp.bfloat16)
        for h in range(H):
            slot_ref[j * TILE : (j + 1) * TILE, h * HD : (h + 1) * HD] = merged[h * TILE : (h + 1) * TILE]
    block, cut = outs[0].shape
    placed = sum(dot(back_ref[f], slot_ref[:, f * cut : (f + 1) * cut]) for f in range(fold))
    placed = placed.astype(jnp.bfloat16)
    for d, out in enumerate(outs):
        out[...] = placed[d * block : (d + 1) * block]


def unroute_kernel(*refs):
    blocks, back_ref, out = refs[:-2], refs[-2], refs[-1]
    width = blocks[0].shape[1]
    joined = jnp.concatenate([b[...] for b in reversed(blocks)], axis=0)
    for f in range(back_ref.shape[0]):
        out[:, f * width : (f + 1) * width] = dot(back_ref[f], joined).astype(jnp.bfloat16)


def swapped(block, axis, distance):
    devices = range(lax.axis_size(axis))
    return lax.ppermute(block, axis, [(i, i ^ distance) for i in devices])


def per_device(queries, q_pos, req_of, cache, cache_len):
    tok_rows = queries.shape[0]
    groups = lax.axis_size("req")
    cycle = lax.axis_size("ctx")
    chips = cycle // 2
    capacity = 5 * tok_rows // (4 * groups)
    slots = groups * capacity
    fold = fold_of(capacity)
    block, width = capacity * fold, WIDE // fold
    shard_len = cache.shape[1]
    half = shard_len // 2
    here = lax.axis_index("ctx")
    mine = lax.axis_index("req")
    me = jnp.stack([here, mine]).astype(jnp.int32)
    bf = lambda *shape: jax.ShapeDtypeStruct(shape, jnp.bfloat16)

    *sends, back_tok, kept, away = call(
        functools.partial(route_kernel, capacity),
        [bf(block, width + META)] * groups + [bf(fold, tok_rows, groups * block)] + [bf(half, 2 * HD)] * 2,
        [SMEM] + [pl.BlockSpec(memory_space=pltpu.HBM)] * 4,
        "route",
        scratch=[
            pltpu.VMEM((1, tok_rows), jnp.int32),
            pltpu.VMEM((1, tok_rows), jnp.int32),
            pltpu.VMEM((tok_rows, WIDE), jnp.bfloat16),
            pltpu.SemaphoreType.DMA((5,)),
        ],
    )(me, *[in_hbm(x) for x in (req_of.reshape(1, tok_rows), q_pos.reshape(1, tok_rows), queries, cache[0])])
    blocks = {d: swapped(sends[d], "req", d) for d in reversed(range(1, groups))}
    blocks[0] = sends[0]
    away = swapped(away, "ctx", cycle - 2)
    kept_sib = swapped(kept, "ctx", 1)
    all_keys = [bf(4 * half, 2 * HD), bf(HD + 16, 4 * half)]
    kept_keys = call(functools.partial(keys_kernel, 0, (1, 1)), all_keys, [VMEM] * 2, "kept_keys")(kept, kept_sib)
    blocks[0], *kept_keys = lax.optimization_barrier((blocks[0], *kept_keys))

    sorted_q, back_slot = call(
        functools.partial(sort_kernel, capacity),
        [bf(slots, WIDE + META), bf(fold, groups * block, slots)],
        [VMEM] * groups,
        "sort",
    )(*[blocks[d] for d in reversed(range(groups))])
    visiting = {d: swapped(sorted_q, "ctx", 2 * d) for d in range(1, chips)}
    sorted_q, away = lax.optimization_barrier((sorted_q, away))
    away_sib = [swapped(away[i * half // 2 : (i + 1) * half // 2], "ctx", 1) for i in range(2)]

    k_all, vt_all = call(
        functools.partial(keys_kernel, 2, (1, 2)), all_keys, [VMEM] * 5, "away_keys", aliases={3: 0, 4: 1}
    )(away, *away_sib, *kept_keys)

    def flash(q, first=0, tiles=slots // TILE):
        extra = (tiles + 1) * TILE * H
        return call(
            functools.partial(flash_kernel, first, chips, half),
            bf(OUT_ROWS, tiles * TILE * H),
            [SMEM, SMEM] + [VMEM] * 3,
            "flash",
            scratch=[
                pltpu.VMEM((extra, 2 * HD), jnp.bfloat16),
                pltpu.VMEM((HD + 16, extra), jnp.float32),
                pltpu.VMEM((8, extra), jnp.float32),
                pltpu.VMEM((2, SUB, TILE * H), jnp.float32),
                pltpu.VMEM((8, tiles * TILE * H), jnp.float32),
                pltpu.SMEM((2 * tiles + 4,), jnp.int32),
                pltpu.SMEM((8,), jnp.int32),
            ],
        )(me, cache_len, q, k_all, vt_all)

    turn = flash(sorted_q, 0, 2)
    own = [turn]
    home = []
    for d in sorted(visiting, key=lambda d: (d & (d - 1) != 0, d)):
        turn, q = lax.optimization_barrier((turn, visiting[d]))
        turn = flash(q)
        home.append(swapped(turn, "ctx", 2 * d))
    turn, q, *home[:-1] = lax.optimization_barrier((turn, sorted_q, *home[:-1]))
    own.append(flash(q, 2, slots // TILE - 2))
    home = [*own, *home]
    outs = call(
        functools.partial(merge_kernel, len(home) - 2),
        [bf(block, width)] * groups,
        [VMEM] * (len(home) + 1),
        "merge",
        scratch=[pltpu.VMEM((slots, WIDE), jnp.bfloat16)],
    )(*home, back_slot)
    back = [swapped(outs[d], "req", d) for d in reversed(range(1, groups))] + [outs[0]]
    return call(unroute_kernel, bf(tok_rows, WIDE), [VMEM] * (groups + 1), "unroute")(*back, back_tok)


def solution(mesh):
    in_specs = (
        P(("ctx", "req"), None),
        P(("ctx", "req")),
        P(("ctx", "req"), None),
        P("req", "ctx", None),
        P(),
    )
    out_specs = P(("ctx", "req"), None)
    return jax.shard_map(
        per_device, mesh=mesh, in_specs=in_specs, out_specs=out_specs, check_vma=False
    )
```

```python
import functools
import math

import jax
import jax.numpy as jnp
from jax import lax
from jax.experimental import pallas as pl
from jax.experimental.pallas import tpu as pltpu
from jax.sharding import PartitionSpec as P

H = 16
HD = 128
WIDE = H * HD
META = 128
LOW = -1e30
TILE = 16
SUB = 256
OUT_ROWS = HD + 8
EXP_SCALE = HD**-0.5 * math.log2(math.e)
NT = (((1,), (1,)), ((), ()))
NN = (((1,), (0,)), ((), ()))
VMEM = pl.BlockSpec(memory_space=pltpu.VMEM)
SMEM = pl.BlockSpec(memory_space=pltpu.SMEM)


def dot(a, b, dims=NN):
    return lax.dot_general(a, b, dims, preferred_element_type=jnp.float32)


def in_hbm(x):
    return pltpu.with_memory_space_constraint(x, pltpu.HBM)


def iota(shape, dim):
    return lax.broadcasted_iota(jnp.int32, shape, dim)


def row_of(column):
    return jnp.transpose(jnp.broadcast_to(column, (column.shape[0], 128)), (1, 0))[:1, :]


def call(body, out_shape, in_specs, name, scratch=(), limit=20, aliases=None):
    many = isinstance(out_shape, list)
    return pl.pallas_call(
        body,
        out_shape=out_shape,
        in_specs=in_specs,
        out_specs=[VMEM] * len(out_shape) if many else VMEM,
        scratch_shapes=list(scratch),
        compiler_params=pltpu.CompilerParams(vmem_limit_bytes=limit << 20),
        cost_estimate=pl.CostEstimate(flops=1, bytes_accessed=1, transcendentals=0),
        input_output_aliases=aliases or {},
        name=name,
    )


def fold_of(capacity):
    fold = 1
    while capacity * fold % 8:
        fold *= 2
    return fold


def route_kernel(capacity, me_ref, req_hbm, pos_hbm, q_hbm, shard_hbm, *outs):
    outs, (req_ref, pos_ref, q_ref, sem) = outs[:-4], outs[-4:]
    sends, back_ref, halves = outs[:-3], outs[-3], outs[-2:]
    half = halves[0].shape[0]
    moves = [(req_hbm, req_ref), (pos_hbm, pos_ref), (q_hbm, q_ref)]
    moves += [(shard_hbm.at[pl.ds(i * half, half)], halves[i]) for i in range(2)]
    fetches = [pltpu.make_async_copy(src, dst, sem.at[i]) for i, (src, dst) in enumerate(moves)]
    for fetch in fetches:
        fetch.start()
    for fetch in fetches[:3]:
        fetch.wait()
    rows = q_ref.shape[0]
    fold = fold_of(capacity)
    block, width = capacity * fold, WIDE // fold
    i0, i1 = iota((rows, rows), 0), iota((rows, rows), 1)
    target_r = req_ref[...]
    target_c = jnp.sum(jnp.where(i0 == i1, target_r, 0), axis=1, keepdims=True)
    same = target_c == target_r
    rank_c = jnp.sum((same & (i1 < i0)).astype(jnp.int32), axis=1, keepdims=True)
    rank_r = jnp.sum((same & (i0 < i1)).astype(jnp.int32), axis=0, keepdims=True)
    slot_c = (target_c ^ me_ref[1]) * block + rank_c
    slot_r = (target_r ^ me_ref[1]) * block + rank_r
    total = len(sends) * block
    moved = jnp.zeros((total, width), jnp.float32)
    taken = jnp.zeros((total, rows), jnp.float32)
    for f in range(fold):
        back_ref[f] = (slot_c + f * capacity == iota((rows, total), 1)).astype(jnp.bfloat16)
        place = (slot_r + f * capacity == iota((total, rows), 0)).astype(jnp.float32)
        moved += dot(place.astype(jnp.bfloat16), q_ref[:, f * width : (f + 1) * width])
        taken += place
    plus = pos_ref[...] + 1
    high = jnp.sum(taken * (plus >> 8).astype(jnp.float32), axis=1, keepdims=True)
    low = jnp.sum(taken * (plus & 255).astype(jnp.float32), axis=1, keepdims=True)
    lane = iota((total, META), 1)
    meta = jnp.where(lane == 0, high, jnp.where(lane == 1, low, 0.0)).astype(jnp.bfloat16)
    moved = moved.astype(jnp.bfloat16)
    for d, out in enumerate(sends):
        out[:, :width] = moved[d * block : (d + 1) * block]
        out[:, width:] = meta[d * block : (d + 1) * block]
    for fetch in fetches[3:]:
        fetch.wait()


def row_parts(shape, dim, capacity):
    fold = fold_of(capacity)
    row = iota(shape, dim)
    token = jnp.zeros(shape, jnp.int32)
    part = jnp.zeros(shape, jnp.int32)
    for i in range(1, shape[dim] // capacity):
        passed = (row >= i * capacity).astype(jnp.int32)
        part += passed if i % fold else (1 - fold) * passed
    token = row - part * capacity
    for i in range(1, shape[dim] // (capacity * fold)):
        token -= (row >= i * capacity * fold).astype(jnp.int32) * (capacity * fold - capacity)
    return token, part


def sort_kernel(capacity, *refs):
    blocks, out, back_ref = refs[:-2], refs[-2], refs[-1]
    slots = out.shape[0]
    fold = fold_of(capacity)
    width = WIDE // fold
    joined = jnp.concatenate([b[...] for b in reversed(blocks)], axis=0)
    total = joined.shape[0]
    meta = joined[:, width:].astype(jnp.float32)
    pos_c = meta[:, 0:1] * 256.0 + meta[:, 1:2]
    pos_r = row_of(pos_c)
    token_c, part_c = row_parts((total, 1), 0, capacity)
    token_r, part_r = row_parts((1, total), 1, capacity)
    ahead_r = ((pos_c > pos_r) | ((pos_c == pos_r) & (token_c < token_r))) & (part_c == 0)
    ahead_c = ((pos_r > pos_c) | ((pos_r == pos_c) & (token_r < token_c))) & (part_r == 0)
    rank_r = jnp.sum(ahead_r.astype(jnp.int32), axis=0, keepdims=True)
    rank_c = jnp.sum(ahead_c.astype(jnp.int32), axis=1, keepdims=True)
    place = rank_r == iota((slots, total), 0)
    for f in range(fold):
        mine = (place & (part_r == f)).astype(jnp.bfloat16)
        out[:, f * width : (f + 1) * width] = dot(mine, joined[:, :width]).astype(jnp.bfloat16)
        if f == 0:
            out[:, WIDE:] = dot(mine, joined[:, width:]).astype(jnp.bfloat16)
        back_ref[f] = ((rank_c == iota((total, slots), 1)) & (part_c == f)).astype(jnp.bfloat16)


def store_keys(k_ref, vt_ref, number, piece):
    count = piece.shape[0]
    at = slice(number * count, (number + 1) * count)
    k_ref[at, :HD] = piece[:, :HD]
    k_ref[at, HD:] = piece[:, :HD]
    vt_ref[:HD, at] = jnp.transpose(piece[:, HD:], (1, 0))
    vt_ref[HD:, at] = (iota((vt_ref.shape[0] - HD, count), 0) == 0).astype(jnp.bfloat16)


def keys_kernel(first, pieces, *refs):
    k_ref, vt_ref = refs[-2:]
    at = 0
    for number, count in enumerate(pieces, first):
        store_keys(k_ref, vt_ref, number, jnp.concatenate([ref[...] for ref in refs[at : at + count]], axis=0))
        at += count


def flash_kernel(
    first, chips, piece, me_ref, len_ref, pq_ref, k_ref, vt_ref, out_ref, q_ref, acc_ref, row_ref, s_ref, top_ref, job_ref, info_ref
):
    width = TILE * H
    all_width = out_ref.shape[1]
    tiles = all_width // width
    pieces = 4
    length = len_ref[me_ref[1]]
    chip, core = me_ref[0] // 2, lax.rem(me_ref[0], 2)
    home_at = chip * (4 * piece)
    away_at = (chips - 1 - chip) * (4 * piece) + piece
    rising = home_at < away_at
    for pair, kept in enumerate((rising, jnp.logical_not(rising))):
        for k in range(2):
            info_ref[2 * pair + k] = jnp.where(kept, home_at, away_at) + 2 * piece * k
            info_ref[pieces + 2 * pair + k] = jnp.where(kept, 0, 2) + jnp.where(core == k, 0, 1)
    meta = pq_ref[first * TILE : (first + tiles) * TILE, WIDE:].astype(jnp.float32)
    pos = meta[:, 0:1] * 256.0 + meta[:, 1:2] - 1.0
    last = jnp.minimum(pos, (length - 1).astype(jnp.float32))
    tops, lows = [], []
    for j in range(tiles):
        here = last[j * TILE : (j + 1) * TILE]
        tops.append(jnp.max(here).astype(jnp.int32))
        lows.append(jnp.min(here).astype(jnp.int32))
        row_ref[0:1, j * width : (j + 1) * width] = jnp.concatenate([row_of(here)] * H, axis=1)
        rows = slice((first + j) * TILE, (first + j + 1) * TILE)
        for h in range(H):
            x = pq_ref[rows, h * HD : (h + 1) * HD].astype(jnp.float32) * EXP_SCALE
            high = x.astype(jnp.bfloat16)
            at = slice(j * width + h * TILE, j * width + (h + 1) * TILE)
            q_ref[at, :HD] = high
            q_ref[at, HD:] = (x - high.astype(jnp.float32)).astype(jnp.bfloat16)
    count, whole = jnp.int32(0), []
    for j in range(tiles):
        for i in range(pieces):
            whole.append(info_ref[i] + (piece - 1) <= lows[j])
            job_ref[count] = j * pieces + i
            count += whole[-1].astype(jnp.int32)
    whole_turns = count // 2
    for j in range(tiles):
        for i in range(pieces):
            job_ref[count] = j * pieces + i
            count += ((info_ref[i] <= tops[j]) & jnp.logical_not(whole[j * pieces + i])).astype(jnp.int32)
    for k in range(3):
        job_ref[count + k] = tiles * pieces
    row_ref[0:1, all_width:] = jnp.full((1, width), -1.0, jnp.float32)
    q_ref[all_width:, :] = jnp.zeros((width, 2 * HD), jnp.bfloat16)
    acc_ref[...] = jnp.zeros_like(acc_ref)

    def place(job):
        tile = job // pieces
        return pl.ds(pl.multiple_of(tile * width, width), width), job - tile * pieces

    def keys(c, a, n):
        return pl.ds(pl.multiple_of(info_ref[pieces + c] * piece + a, 128), n)

    def scores(cols, c, a, n):
        return dot(k_ref[keys(c, a, n), :], q_ref[cols, :], NT)

    def masked(s, cols, c, a):
        limit = row_ref[0:1, cols].astype(jnp.int32) - (info_ref[c] + a)
        return jnp.where(iota(s.shape, 0) <= limit, s, LOW)

    subs = [(0, SUB), (SUB, piece - SUB)]

    @pl.when(count > 0)
    def _():
        for k in range(2):
            cols, c = place(job_ref[k])
            s_ref[k] = scores(cols, c, *subs[0])

    def turn(b, mask):
        now = [place(job_ref[2 * b + k]) for k in range(2)]
        later = [place(job_ref[2 * b + 2 + k]) for k in range(2)]
        s = [s_ref[k] for k in range(2)]
        totals = [None, None]
        for i, (a, n) in enumerate(subs):
            if i + 1 < len(subs):
                next_s = [scores(cols, c, *subs[i + 1]) for cols, c in now]
            else:
                next_s = [scores(cols, c, *subs[0]) for cols, c in later]
            for k, (cols, c) in enumerate(now):
                weights = jnp.exp2(masked(s[k], cols, c, a) if mask else s[k]).astype(jnp.bfloat16)
                term = dot(vt_ref[:, keys(c, a, n)], weights)
                totals[k] = term if totals[k] is None else totals[k] + term
            s = next_s
        for k in range(2):
            s_ref[k] = s[k]
        for k, (cols, _) in enumerate(now):
            acc_ref[:, cols] += totals[k]

    pl.loop(0, whole_turns)(lambda b: turn(b, False))
    pl.loop(whole_turns, (count + 1) // 2)(lambda b: turn(b, True))
    top_ref[0:1, :] = jnp.zeros((1, all_width), jnp.float32)
    total = acc_ref[HD : HD + 1, :all_width]
    dead = row_ref[0:1, :all_width] < info_ref[0].astype(jnp.float32)
    fine = dead | ((total > 2.0**-60) & (total < 2.0**100))

    @pl.when(jnp.logical_not(jnp.min(fine.astype(jnp.float32)) > 0.5))
    def _():
        acc_ref[...] = jnp.zeros_like(acc_ref)
        top_ref[0:1, :] = jnp.full((1, all_width), 0.1 * LOW, jnp.float32)

        def careful(i, carry):
            chunks = piece // 128
            cols = pl.ds(pl.multiple_of(i // (pieces * chunks) * width, width), width)
            c, a = i % (pieces * chunks) // chunks, i % chunks * 128
            s = masked(scores(cols, c, a, 128), cols, c, a)
            before = top_ref[0:1, cols]
            after = jnp.maximum(before, jnp.max(s, axis=0, keepdims=True))
            weights = jnp.exp2(s - after).astype(jnp.bfloat16)
            acc_ref[:, cols] = acc_ref[:, cols] * jnp.exp2(before - after) + dot(vt_ref[:, keys(c, a, 128)], weights)
            top_ref[0:1, cols] = after
            return carry

        lax.fori_loop(0, tiles * pieces * (piece // 128), careful, 0)

    total = acc_ref[HD : HD + 1, :all_width]
    some = total > 0.0
    safe = jnp.where(some, total, 1.0)
    out_ref[:HD, :] = (acc_ref[:HD, :all_width] * (1.0 / safe)).astype(jnp.bfloat16)
    lse = jnp.where(some, top_ref[0:1, :] + jnp.log2(safe), LOW)
    a = lse.astype(jnp.bfloat16).astype(jnp.float32)
    b = (lse - a).astype(jnp.bfloat16).astype(jnp.float32)
    row = iota((OUT_ROWS - HD, all_width), 0)
    terms = jnp.where(row == 0, a, jnp.where(row == 1, b, jnp.where(row == 2, lse - a - b, 0.0)))
    out_ref[HD:, :] = terms.astype(jnp.bfloat16)


def merge_kernel(cuts, *refs):
    count = sum(cuts)
    pieces, back_ref, outs, slot_ref = list(refs[:count]), refs[count], refs[count + 1 : -1], refs[-1]
    fold = back_ref.shape[0]
    width = TILE * H
    parts = []
    for cut in cuts:
        taken, pieces = pieces[:cut], pieces[cut:]
        parts.append([(ref, slice(i, i + width)) for ref in taken for i in range(0, ref.shape[1], width)])
    for j in range(slot_ref.shape[0] // TILE):
        here = [part[j] for part in parts]
        lses = [sum(part[HD + i : HD + i + 1, cols].astype(jnp.float32) for i in range(3)) for part, cols in here]
        high = functools.reduce(jnp.maximum, lses)
        shares = [jnp.exp2(lse - high) for lse in lses]
        scale = 1.0 / functools.reduce(jnp.add, shares)
        merged = sum((share * scale) * part[:HD, cols].astype(jnp.float32) for share, (part, cols) in zip(shares, here))
        merged = jnp.transpose(merged, (1, 0)).astype(jnp.bfloat16)
        for h in range(H):
            slot_ref[j * TILE : (j + 1) * TILE, h * HD : (h + 1) * HD] = merged[h * TILE : (h + 1) * TILE]
    block, cut = outs[0].shape
    placed = sum(dot(back_ref[f], slot_ref[:, f * cut : (f + 1) * cut]) for f in range(fold))
    placed = placed.astype(jnp.bfloat16)
    for d, out in enumerate(outs):
        out[...] = placed[d * block : (d + 1) * block]


def unroute_kernel(*refs):
    blocks, back_ref, out = refs[:-2], refs[-2], refs[-1]
    width = blocks[0].shape[1]
    joined = jnp.concatenate([b[...] for b in reversed(blocks)], axis=0)
    for f in range(back_ref.shape[0]):
        out[:, f * width : (f + 1) * width] = dot(back_ref[f], joined).astype(jnp.bfloat16)


def swapped(block, axis, distance):
    devices = range(lax.axis_size(axis))
    return lax.ppermute(block, axis, [(i, i ^ distance) for i in devices])


def per_device(queries, q_pos, req_of, cache, cache_len):
    tok_rows = queries.shape[0]
    groups = lax.axis_size("req")
    cycle = lax.axis_size("ctx")
    chips = cycle // 2
    capacity = 5 * tok_rows // (4 * groups)
    slots = groups * capacity
    fold = fold_of(capacity)
    block, width = capacity * fold, WIDE // fold
    shard_len = cache.shape[1]
    half = shard_len // 2
    here = lax.axis_index("ctx")
    mine = lax.axis_index("req")
    me = jnp.stack([here, mine]).astype(jnp.int32)
    bf = lambda *shape: jax.ShapeDtypeStruct(shape, jnp.bfloat16)

    *sends, back_tok, kept, away = call(
        functools.partial(route_kernel, capacity),
        [bf(block, width + META)] * groups + [bf(fold, tok_rows, groups * block)] + [bf(half, 2 * HD)] * 2,
        [SMEM] + [pl.BlockSpec(memory_space=pltpu.HBM)] * 4,
        "route",
        scratch=[
            pltpu.VMEM((1, tok_rows), jnp.int32),
            pltpu.VMEM((1, tok_rows), jnp.int32),
            pltpu.VMEM((tok_rows, WIDE), jnp.bfloat16),
            pltpu.SemaphoreType.DMA((5,)),
        ],
    )(me, *[in_hbm(x) for x in (req_of.reshape(1, tok_rows), q_pos.reshape(1, tok_rows), queries, cache[0])])
    blocks = {d: swapped(sends[d], "req", d) for d in reversed(range(1, groups))}
    blocks[0] = sends[0]
    away = swapped(away, "ctx", cycle - 2)
    kept_sib = swapped(kept, "ctx", 1)
    all_keys = [bf(4 * half, 2 * HD), bf(HD + 16, 4 * half)]
    kept_keys = call(functools.partial(keys_kernel, 0, (1, 1)), all_keys, [VMEM] * 2, "kept_keys")(kept, kept_sib)
    blocks[0], *kept_keys = lax.optimization_barrier((blocks[0], *kept_keys))

    sorted_q, back_slot = call(
        functools.partial(sort_kernel, capacity),
        [bf(slots, WIDE + META), bf(fold, groups * block, slots)],
        [VMEM] * groups,
        "sort",
    )(*[blocks[d] for d in reversed(range(groups))])
    visiting = {d: swapped(sorted_q, "ctx", 2 * d) for d in range(1, chips)}
    sorted_q, away = lax.optimization_barrier((sorted_q, away))
    away_sib = [swapped(away[i * half // 2 : (i + 1) * half // 2], "ctx", 1) for i in range(2)]

    k_all, vt_all = call(
        functools.partial(keys_kernel, 2, (1, 2)), all_keys, [VMEM] * 5, "away_keys", aliases={3: 0, 4: 1}
    )(away, *away_sib, *kept_keys)

    def flash(q, first=0, tiles=slots // TILE):
        extra = (tiles + 1) * TILE * H
        return call(
            functools.partial(flash_kernel, first, chips, half),
            bf(OUT_ROWS, tiles * TILE * H),
            [SMEM, SMEM] + [VMEM] * 3,
            "flash",
            scratch=[
                pltpu.VMEM((extra, 2 * HD), jnp.bfloat16),
                pltpu.VMEM((HD + 16, extra), jnp.float32),
                pltpu.VMEM((8, extra), jnp.float32),
                pltpu.VMEM((2, SUB, TILE * H), jnp.float32),
                pltpu.VMEM((8, tiles * TILE * H), jnp.float32),
                pltpu.SMEM((4 * tiles + 4,), jnp.int32),
                pltpu.SMEM((8,), jnp.int32),
            ],
        )(me, cache_len, q, k_all, vt_all)

    tiles = slots // TILE
    last = max(visiting, key=lambda d: (d & (d - 1) != 0, d))
    turn = flash(sorted_q, 0, 2)
    own, home = [turn], {}
    for d in sorted(visiting, key=lambda d: (d == last, d & (d - 1) != 0, d)):
        home[d] = []
        for at, count in ((0, 3), (3, tiles - 3)) if d == last else ((0, tiles),):
            turn, q = lax.optimization_barrier((turn, visiting[d]))
            turn = flash(q, at, count)
            home[d].append(swapped(turn, "ctx", 2 * d))
    before = [home[d][0] for d in home if d != last]
    turn, q, *before = lax.optimization_barrier((turn, sorted_q, *before))
    own.append(flash(q, 2, tiles - 2))
    home = [own, home[last], *[[part] for part in before]]
    cuts = tuple(len(part) for part in home)
    home = [ref for part in home for ref in part]
    outs = call(
        functools.partial(merge_kernel, cuts),
        [bf(block, width)] * groups,
        [VMEM] * (len(home) + 1),
        "merge",
        scratch=[pltpu.VMEM((slots, WIDE), jnp.bfloat16)],
    )(*home, back_slot)
    back = [swapped(outs[d], "req", d) for d in reversed(range(1, groups))] + [outs[0]]
    return call(unroute_kernel, bf(tok_rows, WIDE), [VMEM] * (groups + 1), "unroute")(*back, back_tok)


def solution(mesh):
    in_specs = (
        P(("ctx", "req"), None),
        P(("ctx", "req")),
        P(("ctx", "req"), None),
        P("req", "ctx", None),
        P(),
    )
    out_specs = P(("ctx", "req"), None)
    return jax.shard_map(
        per_device, mesh=mesh, in_specs=in_specs, out_specs=out_specs, check_vma=False
    )
```

```python
import functools
import math

import jax
import jax.numpy as jnp
from jax import lax
from jax.experimental import pallas as pl
from jax.experimental.pallas import tpu as pltpu
from jax.sharding import PartitionSpec as P

H = 16
HD = 128
WIDE = H * HD
META = 128
LOW = -1e30
TILE = 16
SUB = 256
OUT_ROWS = HD + 8
EXP_SCALE = HD**-0.5 * math.log2(math.e)
NT = (((1,), (1,)), ((), ()))
NN = (((1,), (0,)), ((), ()))
VMEM = pl.BlockSpec(memory_space=pltpu.VMEM)
SMEM = pl.BlockSpec(memory_space=pltpu.SMEM)


def dot(a, b, dims=NN):
    return lax.dot_general(a, b, dims, preferred_element_type=jnp.float32)


def in_hbm(x):
    return pltpu.with_memory_space_constraint(x, pltpu.HBM)


def iota(shape, dim):
    return lax.broadcasted_iota(jnp.int32, shape, dim)


def row_of(column):
    return jnp.transpose(jnp.broadcast_to(column, (column.shape[0], 128)), (1, 0))[:1, :]


def call(body, out_shape, in_specs, name, scratch=(), limit=20, aliases=None):
    many = isinstance(out_shape, list)
    return pl.pallas_call(
        body,
        out_shape=out_shape,
        in_specs=in_specs,
        out_specs=[VMEM] * len(out_shape) if many else VMEM,
        scratch_shapes=list(scratch),
        compiler_params=pltpu.CompilerParams(vmem_limit_bytes=limit << 20),
        cost_estimate=pl.CostEstimate(flops=1, bytes_accessed=1, transcendentals=0),
        input_output_aliases=aliases or {},
        name=name,
    )


def fold_of(capacity):
    fold = 1
    while capacity * fold % 8:
        fold *= 2
    return fold


def route_kernel(capacity, me_ref, req_hbm, pos_hbm, q_hbm, shard_hbm, *outs):
    outs, (req_ref, pos_ref, q_ref, sem) = outs[:-4], outs[-4:]
    sends, back_ref, halves = outs[:-3], outs[-3], outs[-2:]
    half = halves[0].shape[0]
    moves = [(req_hbm, req_ref), (pos_hbm, pos_ref), (q_hbm, q_ref)]
    moves += [(shard_hbm.at[pl.ds(i * half, half)], halves[i]) for i in range(2)]
    fetches = [pltpu.make_async_copy(src, dst, sem.at[i]) for i, (src, dst) in enumerate(moves)]
    for fetch in fetches:
        fetch.start()
    for fetch in fetches[:3]:
        fetch.wait()
    rows = q_ref.shape[0]
    fold = fold_of(capacity)
    block, width = capacity * fold, WIDE // fold
    i0, i1 = iota((rows, rows), 0), iota((rows, rows), 1)
    target_r = req_ref[...]
    target_c = jnp.sum(jnp.where(i0 == i1, target_r, 0), axis=1, keepdims=True)
    same = target_c == target_r
    rank_c = jnp.sum((same & (i1 < i0)).astype(jnp.int32), axis=1, keepdims=True)
    rank_r = jnp.sum((same & (i0 < i1)).astype(jnp.int32), axis=0, keepdims=True)
    slot_c = (target_c ^ me_ref[1]) * block + rank_c
    slot_r = (target_r ^ me_ref[1]) * block + rank_r
    total = len(sends) * block
    moved = jnp.zeros((total, width), jnp.float32)
    taken = jnp.zeros((total, rows), jnp.float32)
    for f in range(fold):
        back_ref[f] = (slot_c + f * capacity == iota((rows, total), 1)).astype(jnp.bfloat16)
        place = (slot_r + f * capacity == iota((total, rows), 0)).astype(jnp.float32)
        moved += dot(place.astype(jnp.bfloat16), q_ref[:, f * width : (f + 1) * width])
        taken += place
    plus = pos_ref[...] + 1
    high = jnp.sum(taken * (plus >> 8).astype(jnp.float32), axis=1, keepdims=True)
    low = jnp.sum(taken * (plus & 255).astype(jnp.float32), axis=1, keepdims=True)
    lane = iota((total, META), 1)
    meta = jnp.where(lane == 0, high, jnp.where(lane == 1, low, 0.0)).astype(jnp.bfloat16)
    moved = moved.astype(jnp.bfloat16)
    for d, out in enumerate(sends):
        out[:, :width] = moved[d * block : (d + 1) * block]
        out[:, width:] = meta[d * block : (d + 1) * block]
    for fetch in fetches[3:]:
        fetch.wait()


def row_parts(shape, dim, capacity):
    fold = fold_of(capacity)
    row = iota(shape, dim)
    token = jnp.zeros(shape, jnp.int32)
    part = jnp.zeros(shape, jnp.int32)
    for i in range(1, shape[dim] // capacity):
        passed = (row >= i * capacity).astype(jnp.int32)
        part += passed if i % fold else (1 - fold) * passed
    token = row - part * capacity
    for i in range(1, shape[dim] // (capacity * fold)):
        token -= (row >= i * capacity * fold).astype(jnp.int32) * (capacity * fold - capacity)
    return token, part


def sort_kernel(capacity, *refs):
    blocks, out, back_ref = refs[:-2], refs[-2], refs[-1]
    slots = out.shape[0]
    fold = fold_of(capacity)
    width = WIDE // fold
    joined = jnp.concatenate([b[...] for b in reversed(blocks)], axis=0)
    total = joined.shape[0]
    meta = joined[:, width:].astype(jnp.float32)
    pos_c = meta[:, 0:1] * 256.0 + meta[:, 1:2]
    pos_r = row_of(pos_c)
    token_c, part_c = row_parts((total, 1), 0, capacity)
    token_r, part_r = row_parts((1, total), 1, capacity)
    ahead_r = ((pos_c > pos_r) | ((pos_c == pos_r) & (token_c < token_r))) & (part_c == 0)
    ahead_c = ((pos_r > pos_c) | ((pos_r == pos_c) & (token_r < token_c))) & (part_r == 0)
    rank_r = jnp.sum(ahead_r.astype(jnp.int32), axis=0, keepdims=True)
    rank_c = jnp.sum(ahead_c.astype(jnp.int32), axis=1, keepdims=True)
    place = rank_r == iota((slots, total), 0)
    for f in range(fold):
        mine = (place & (part_r == f)).astype(jnp.bfloat16)
        out[:, f * width : (f + 1) * width] = dot(mine, joined[:, :width]).astype(jnp.bfloat16)
        if f == 0:
            out[:, WIDE:] = dot(mine, joined[:, width:]).astype(jnp.bfloat16)
        back_ref[f] = ((rank_c == iota((total, slots), 1)) & (part_c == f)).astype(jnp.bfloat16)


def store_keys(k_ref, vt_ref, number, piece):
    count = piece.shape[0]
    at = slice(number * count, (number + 1) * count)
    k_ref[at, :HD] = piece[:, :HD]
    k_ref[at, HD:] = piece[:, :HD]
    vt_ref[:HD, at] = jnp.transpose(piece[:, HD:], (1, 0))
    vt_ref[HD:, at] = (iota((vt_ref.shape[0] - HD, count), 0) == 0).astype(jnp.bfloat16)


def keys_kernel(first, pieces, *refs):
    k_ref, vt_ref = refs[-2:]
    at = 0
    for number, count in enumerate(pieces, first):
        store_keys(k_ref, vt_ref, number, jnp.concatenate([ref[...] for ref in refs[at : at + count]], axis=0))
        at += count


def flash_kernel(
    first, chips, piece, me_ref, len_ref, pq_ref, k_ref, vt_ref, out_ref, q_ref, acc_ref, row_ref, s_ref, top_ref, job_ref, info_ref
):
    width = TILE * H
    all_width = out_ref.shape[1]
    tiles = all_width // width
    pieces = 4
    length = len_ref[me_ref[1]]
    chip, core = me_ref[0] // 2, lax.rem(me_ref[0], 2)
    home_at = chip * (4 * piece)
    away_at = (chips - 1 - chip) * (4 * piece) + piece
    rising = home_at < away_at
    for pair, kept in enumerate((rising, jnp.logical_not(rising))):
        for k in range(2):
            info_ref[2 * pair + k] = jnp.where(kept, home_at, away_at) + 2 * piece * k
            info_ref[pieces + 2 * pair + k] = jnp.where(kept, 0, 2) + jnp.where(core == k, 0, 1)
    meta = pq_ref[first * TILE : (first + tiles) * TILE, WIDE:].astype(jnp.float32)
    pos = meta[:, 0:1] * 256.0 + meta[:, 1:2] - 1.0
    last = jnp.minimum(pos, (length - 1).astype(jnp.float32))
    tops, lows = [], []
    for j in range(tiles):
        here = last[j * TILE : (j + 1) * TILE]
        tops.append(jnp.max(here).astype(jnp.int32))
        lows.append(jnp.min(here).astype(jnp.int32))
        row_ref[0:1, j * width : (j + 1) * width] = jnp.concatenate([row_of(here)] * H, axis=1)
        rows = slice((first + j) * TILE, (first + j + 1) * TILE)
        for h in range(H):
            x = pq_ref[rows, h * HD : (h + 1) * HD].astype(jnp.float32) * EXP_SCALE
            high = x.astype(jnp.bfloat16)
            at = slice(j * width + h * TILE, j * width + (h + 1) * TILE)
            q_ref[at, :HD] = high
            q_ref[at, HD:] = (x - high.astype(jnp.float32)).astype(jnp.bfloat16)
    count, whole = jnp.int32(0), []
    for j in range(tiles):
        for i in range(pieces):
            whole.append(info_ref[i] + (piece - 1) <= lows[j])
            job_ref[count] = j * pieces + i
            count += whole[-1].astype(jnp.int32)
    whole_turns = count // 2
    for j in range(tiles):
        for i in range(pieces):
            job_ref[count] = j * pieces + i
            count += ((info_ref[i] <= tops[j]) & jnp.logical_not(whole[j * pieces + i])).astype(jnp.int32)
    for k in range(3):
        job_ref[count + k] = tiles * pieces
    row_ref[0:1, all_width:] = jnp.full((1, width), -1.0, jnp.float32)
    q_ref[all_width:, :] = jnp.zeros((width, 2 * HD), jnp.bfloat16)
    acc_ref[...] = jnp.zeros_like(acc_ref)

    def place(job):
        tile = job // pieces
        return pl.ds(pl.multiple_of(tile * width, width), width), job - tile * pieces

    def keys(c, a, n):
        return pl.ds(pl.multiple_of(info_ref[pieces + c] * piece + a, 128), n)

    def scores(cols, c, a, n):
        return dot(k_ref[keys(c, a, n), :], q_ref[cols, :], NT)

    def masked(s, cols, c, a):
        limit = row_ref[0:1, cols].astype(jnp.int32) - (info_ref[c] + a)
        return jnp.where(iota(s.shape, 0) <= limit, s, LOW)

    subs = [(0, SUB), (SUB, piece - SUB)]

    @pl.when(count > 0)
    def _():
        for k in range(2):
            cols, c = place(job_ref[k])
            s_ref[k] = scores(cols, c, *subs[0])

    def turn(b, mask):
        now = [place(job_ref[2 * b + k]) for k in range(2)]
        later = [place(job_ref[2 * b + 2 + k]) for k in range(2)]
        s = [s_ref[k] for k in range(2)]
        totals = [None, None]
        for i, (a, n) in enumerate(subs):
            if i + 1 < len(subs):
                next_s = [scores(cols, c, *subs[i + 1]) for cols, c in now]
            else:
                next_s = [scores(cols, c, *subs[0]) for cols, c in later]
            for k, (cols, c) in enumerate(now):
                weights = jnp.exp2(masked(s[k], cols, c, a) if mask else s[k]).astype(jnp.bfloat16)
                term = dot(vt_ref[:, keys(c, a, n)], weights)
                totals[k] = term if totals[k] is None else totals[k] + term
            s = next_s
        for k in range(2):
            s_ref[k] = s[k]
        for k, (cols, _) in enumerate(now):
            acc_ref[:, cols] += totals[k]

    pl.loop(0, whole_turns)(lambda b: turn(b, False))
    pl.loop(whole_turns, (count + 1) // 2)(lambda b: turn(b, True))
    top_ref[0:1, :] = jnp.zeros((1, all_width), jnp.float32)
    total = acc_ref[HD : HD + 1, :all_width]
    dead = row_ref[0:1, :all_width] < info_ref[0].astype(jnp.float32)
    fine = dead | ((total > 2.0**-60) & (total < 2.0**100))

    @pl.when(jnp.logical_not(jnp.min(fine.astype(jnp.float32)) > 0.5))
    def _():
        acc_ref[...] = jnp.zeros_like(acc_ref)
        top_ref[0:1, :] = jnp.full((1, all_width), 0.1 * LOW, jnp.float32)

        def careful(i, carry):
            chunks = piece // 128
            cols = pl.ds(pl.multiple_of(i // (pieces * chunks) * width, width), width)
            c, a = i % (pieces * chunks) // chunks, i % chunks * 128
            s = masked(scores(cols, c, a, 128), cols, c, a)
            before = top_ref[0:1, cols]
            after = jnp.maximum(before, jnp.max(s, axis=0, keepdims=True))
            weights = jnp.exp2(s - after).astype(jnp.bfloat16)
            acc_ref[:, cols] = acc_ref[:, cols] * jnp.exp2(before - after) + dot(vt_ref[:, keys(c, a, 128)], weights)
            top_ref[0:1, cols] = after
            return carry

        lax.fori_loop(0, tiles * pieces * (piece // 128), careful, 0)

    total = acc_ref[HD : HD + 1, :all_width]
    some = total > 0.0
    safe = jnp.where(some, total, 1.0)
    out_ref[:HD, :] = (acc_ref[:HD, :all_width] * (1.0 / safe)).astype(jnp.bfloat16)
    lse = jnp.where(some, top_ref[0:1, :] + jnp.log2(safe), LOW)
    a = lse.astype(jnp.bfloat16).astype(jnp.float32)
    b = (lse - a).astype(jnp.bfloat16).astype(jnp.float32)
    row = iota((OUT_ROWS - HD, all_width), 0)
    terms = jnp.where(row == 0, a, jnp.where(row == 1, b, jnp.where(row == 2, lse - a - b, 0.0)))
    out_ref[HD:, :] = terms.astype(jnp.bfloat16)


def merge_kernel(cuts, *refs):
    count = sum(cuts)
    pieces, back_ref, outs, slot_ref = list(refs[:count]), refs[count], refs[count + 1 : -1], refs[-1]
    fold = back_ref.shape[0]
    width = TILE * H
    parts = []
    for cut in cuts:
        taken, pieces = pieces[:cut], pieces[cut:]
        parts.append([(ref, slice(i, i + width)) for ref in taken for i in range(0, ref.shape[1], width)])
    for j in range(slot_ref.shape[0] // TILE):
        here = [part[j] for part in parts]
        lses = [sum(part[HD + i : HD + i + 1, cols].astype(jnp.float32) for i in range(3)) for part, cols in here]
        high = functools.reduce(jnp.maximum, lses)
        shares = [jnp.exp2(lse - high) for lse in lses]
        scale = 1.0 / functools.reduce(jnp.add, shares)
        merged = sum((share * scale) * part[:HD, cols].astype(jnp.float32) for share, (part, cols) in zip(shares, here))
        merged = jnp.transpose(merged, (1, 0)).astype(jnp.bfloat16)
        for h in range(H):
            slot_ref[j * TILE : (j + 1) * TILE, h * HD : (h + 1) * HD] = merged[h * TILE : (h + 1) * TILE]
    block, cut = outs[0].shape
    placed = sum(dot(back_ref[f], slot_ref[:, f * cut : (f + 1) * cut]) for f in range(fold))
    placed = placed.astype(jnp.bfloat16)
    for d, out in enumerate(outs):
        out[...] = placed[d * block : (d + 1) * block]


def unroute_kernel(*refs):
    blocks, back_ref, out = refs[:-2], refs[-2], refs[-1]
    width = blocks[0].shape[1]
    joined = jnp.concatenate([b[...] for b in reversed(blocks)], axis=0)
    for f in range(back_ref.shape[0]):
        out[:, f * width : (f + 1) * width] = dot(back_ref[f], joined).astype(jnp.bfloat16)


def swapped(block, axis, distance):
    devices = range(lax.axis_size(axis))
    return lax.ppermute(block, axis, [(i, i ^ distance) for i in devices])


def per_device(queries, q_pos, req_of, cache, cache_len):
    tok_rows = queries.shape[0]
    groups = lax.axis_size("req")
    cycle = lax.axis_size("ctx")
    chips = cycle // 2
    capacity = 5 * tok_rows // (4 * groups)
    slots = groups * capacity
    fold = fold_of(capacity)
    block, width = capacity * fold, WIDE // fold
    shard_len = cache.shape[1]
    half = shard_len // 2
    here = lax.axis_index("ctx")
    mine = lax.axis_index("req")
    me = jnp.stack([here, mine]).astype(jnp.int32)
    bf = lambda *shape: jax.ShapeDtypeStruct(shape, jnp.bfloat16)

    *sends, back_tok, kept, away = call(
        functools.partial(route_kernel, capacity),
        [bf(block, width + META)] * groups + [bf(fold, tok_rows, groups * block)] + [bf(half, 2 * HD)] * 2,
        [SMEM] + [pl.BlockSpec(memory_space=pltpu.HBM)] * 4,
        "route",
        scratch=[
            pltpu.VMEM((1, tok_rows), jnp.int32),
            pltpu.VMEM((1, tok_rows), jnp.int32),
            pltpu.VMEM((tok_rows, WIDE), jnp.bfloat16),
            pltpu.SemaphoreType.DMA((5,)),
        ],
    )(me, *[in_hbm(x) for x in (req_of.reshape(1, tok_rows), q_pos.reshape(1, tok_rows), queries, cache[0])])
    blocks = {d: swapped(sends[d], "req", d) for d in reversed(range(1, groups))}
    blocks[0] = sends[0]
    away = swapped(away, "ctx", cycle - 2)
    kept_sib = swapped(kept, "ctx", 1)
    all_keys = [bf(4 * half, 2 * HD), bf(HD + 16, 4 * half)]
    kept_keys = call(functools.partial(keys_kernel, 0, (1, 1)), all_keys, [VMEM] * 2, "kept_keys")(kept, kept_sib)
    blocks[0], *kept_keys = lax.optimization_barrier((blocks[0], *kept_keys))

    sorted_q, back_slot = call(
        functools.partial(sort_kernel, capacity),
        [bf(slots, WIDE + META), bf(fold, groups * block, slots)],
        [VMEM] * groups,
        "sort",
    )(*[blocks[d] for d in reversed(range(groups))])
    visiting = {d: swapped(sorted_q, "ctx", 2 * d) for d in range(1, chips)}
    sorted_q, away = lax.optimization_barrier((sorted_q, away))
    away_sib = [swapped(away[i * half // 2 : (i + 1) * half // 2], "ctx", 1) for i in range(2)]

    k_all, vt_all = call(
        functools.partial(keys_kernel, 2, (1, 2)), all_keys, [VMEM] * 5, "away_keys", aliases={3: 0, 4: 1}
    )(away, *away_sib, *kept_keys)

    def flash(q, first=0, tiles=slots // TILE):
        extra = (tiles + 1) * TILE * H
        return call(
            functools.partial(flash_kernel, first, chips, half),
            bf(OUT_ROWS, tiles * TILE * H),
            [SMEM, SMEM] + [VMEM] * 3,
            "flash",
            scratch=[
                pltpu.VMEM((extra, 2 * HD), jnp.bfloat16),
                pltpu.VMEM((HD + 16, extra), jnp.float32),
                pltpu.VMEM((8, extra), jnp.float32),
                pltpu.VMEM((2, SUB, TILE * H), jnp.float32),
                pltpu.VMEM((8, tiles * TILE * H), jnp.float32),
                pltpu.SMEM((4 * tiles + 4,), jnp.int32),
                pltpu.SMEM((8,), jnp.int32),
            ],
        )(me, cache_len, q, k_all, vt_all)

    tiles = slots // TILE
    order = sorted(visiting, key=lambda d: (-d.bit_count(), d))
    last = order[-1]
    turn = flash(sorted_q, 0, 2)
    own, home = [turn], {}
    for d in order:
        home[d] = []
        for at, count in ((0, 3), (3, tiles - 3)) if d == last else ((0, tiles),):
            turn, q = lax.optimization_barrier((turn, visiting[d]))
            turn = flash(q, at, count)
            home[d].append(swapped(turn, "ctx", 2 * d))
    before = [home[d][0] for d in home if d != last]
    turn, q, *before = lax.optimization_barrier((turn, sorted_q, *before))
    own.append(flash(q, 2, tiles - 2))
    home = [own, home[last], *[[part] for part in before]]
    cuts = tuple(len(part) for part in home)
    home = [ref for part in home for ref in part]
    outs = call(
        functools.partial(merge_kernel, cuts),
        [bf(block, width)] * groups,
        [VMEM] * (len(home) + 1),
        "merge",
        scratch=[pltpu.VMEM((slots, WIDE), jnp.bfloat16)],
    )(*home, back_slot)
    back = [swapped(outs[d], "req", d) for d in reversed(range(1, groups))] + [outs[0]]
    return call(unroute_kernel, bf(tok_rows, WIDE), [VMEM] * (groups + 1), "unroute")(*back, back_tok)


def solution(mesh):
    in_specs = (
        P(("ctx", "req"), None),
        P(("ctx", "req")),
        P(("ctx", "req"), None),
        P("req", "ctx", None),
        P(),
    )
    out_specs = P(("ctx", "req"), None)
    return jax.shard_map(
        per_device, mesh=mesh, in_specs=in_specs, out_specs=out_specs, check_vma=False
    )
```

```python
import functools
import math

import jax
import jax.numpy as jnp
from jax import lax
from jax.experimental import pallas as pl
from jax.experimental.pallas import tpu as pltpu
from jax.sharding import PartitionSpec as P

H = 16
HD = 128
WIDE = H * HD
META = 128
LOW = -1e30
TILE = 16
SUB = 256
OUT_ROWS = HD + 8
EXP_SCALE = HD**-0.5 * math.log2(math.e)
NT = (((1,), (1,)), ((), ()))
NN = (((1,), (0,)), ((), ()))
VMEM = pl.BlockSpec(memory_space=pltpu.VMEM)
SMEM = pl.BlockSpec(memory_space=pltpu.SMEM)


def dot(a, b, dims=NN):
    return lax.dot_general(a, b, dims, preferred_element_type=jnp.float32)


def in_hbm(x):
    return pltpu.with_memory_space_constraint(x, pltpu.HBM)


def iota(shape, dim):
    return lax.broadcasted_iota(jnp.int32, shape, dim)


def row_of(column):
    return jnp.transpose(jnp.broadcast_to(column, (column.shape[0], 128)), (1, 0))[:1, :]


def call(body, out_shape, in_specs, name, scratch=(), limit=20, aliases=None):
    many = isinstance(out_shape, list)
    return pl.pallas_call(
        body,
        out_shape=out_shape,
        in_specs=in_specs,
        out_specs=[VMEM] * len(out_shape) if many else VMEM,
        scratch_shapes=list(scratch),
        compiler_params=pltpu.CompilerParams(vmem_limit_bytes=limit << 20),
        cost_estimate=pl.CostEstimate(flops=1, bytes_accessed=1, transcendentals=0),
        input_output_aliases=aliases or {},
        name=name,
    )


def fold_of(capacity):
    fold = 1
    while capacity * fold % 8:
        fold *= 2
    return fold


def route_kernel(capacity, me_ref, req_hbm, pos_hbm, q_hbm, shard_hbm, *outs):
    outs, (req_ref, pos_ref, q_ref, sem) = outs[:-4], outs[-4:]
    sends, back_ref, shard_ref = outs[:-2], outs[-2], outs[-1]
    moves = [(req_hbm, req_ref), (pos_hbm, pos_ref), (q_hbm, q_ref), (shard_hbm, shard_ref)]
    fetches = [pltpu.make_async_copy(src, dst, sem.at[i]) for i, (src, dst) in enumerate(moves)]
    for fetch in fetches:
        fetch.start()
    for fetch in fetches[:3]:
        fetch.wait()
    rows = q_ref.shape[0]
    fold = fold_of(capacity)
    block, width = capacity * fold, WIDE // fold
    i0, i1 = iota((rows, rows), 0), iota((rows, rows), 1)
    target_r = req_ref[...]
    target_c = jnp.sum(jnp.where(i0 == i1, target_r, 0), axis=1, keepdims=True)
    same = target_c == target_r
    rank_c = jnp.sum((same & (i1 < i0)).astype(jnp.int32), axis=1, keepdims=True)
    rank_r = jnp.sum((same & (i0 < i1)).astype(jnp.int32), axis=0, keepdims=True)
    slot_c = (target_c ^ me_ref[1]) * block + rank_c
    slot_r = (target_r ^ me_ref[1]) * block + rank_r
    total = len(sends) * block
    moved = jnp.zeros((total, width), jnp.float32)
    taken = jnp.zeros((total, rows), jnp.float32)
    for f in range(fold):
        back_ref[f] = (slot_c + f * capacity == iota((rows, total), 1)).astype(jnp.bfloat16)
        place = (slot_r + f * capacity == iota((total, rows), 0)).astype(jnp.float32)
        moved += dot(place.astype(jnp.bfloat16), q_ref[:, f * width : (f + 1) * width])
        taken += place
    plus = pos_ref[...] + 1
    high = jnp.sum(taken * (plus >> 8).astype(jnp.float32), axis=1, keepdims=True)
    low = jnp.sum(taken * (plus & 255).astype(jnp.float32), axis=1, keepdims=True)
    lane = iota((total, META), 1)
    meta = jnp.where(lane == 0, high, jnp.where(lane == 1, low, 0.0)).astype(jnp.bfloat16)
    moved = moved.astype(jnp.bfloat16)
    for d, out in enumerate(sends):
        out[:, :width] = moved[d * block : (d + 1) * block]
        out[:, width:] = meta[d * block : (d + 1) * block]
    for fetch in fetches[3:]:
        fetch.wait()


def row_parts(shape, dim, capacity):
    fold = fold_of(capacity)
    row = iota(shape, dim)
    token = jnp.zeros(shape, jnp.int32)
    part = jnp.zeros(shape, jnp.int32)
    for i in range(1, shape[dim] // capacity):
        passed = (row >= i * capacity).astype(jnp.int32)
        part += passed if i % fold else (1 - fold) * passed
    token = row - part * capacity
    for i in range(1, shape[dim] // (capacity * fold)):
        token -= (row >= i * capacity * fold).astype(jnp.int32) * (capacity * fold - capacity)
    return token, part


def sort_kernel(capacity, *refs):
    blocks, out, back_ref = refs[:-2], refs[-2], refs[-1]
    slots = out.shape[0]
    fold = fold_of(capacity)
    width = WIDE // fold
    joined = jnp.concatenate([b[...] for b in reversed(blocks)], axis=0)
    total = joined.shape[0]
    meta = joined[:, width:].astype(jnp.float32)
    pos_c = meta[:, 0:1] * 256.0 + meta[:, 1:2]
    pos_r = row_of(pos_c)
    token_c, part_c = row_parts((total, 1), 0, capacity)
    token_r, part_r = row_parts((1, total), 1, capacity)
    ahead_r = ((pos_c > pos_r) | ((pos_c == pos_r) & (token_c < token_r))) & (part_c == 0)
    ahead_c = ((pos_r > pos_c) | ((pos_r == pos_c) & (token_r < token_c))) & (part_r == 0)
    rank_r = jnp.sum(ahead_r.astype(jnp.int32), axis=0, keepdims=True)
    rank_c = jnp.sum(ahead_c.astype(jnp.int32), axis=1, keepdims=True)
    place = rank_r == iota((slots, total), 0)
    for f in range(fold):
        mine = (place & (part_r == f)).astype(jnp.bfloat16)
        out[:, f * width : (f + 1) * width] = dot(mine, joined[:, :width]).astype(jnp.bfloat16)
        if f == 0:
            out[:, WIDE:] = dot(mine, joined[:, width:]).astype(jnp.bfloat16)
        back_ref[f] = ((rank_c == iota((total, slots), 1)) & (part_c == f)).astype(jnp.bfloat16)


def store_keys(k_ref, vt_ref, number, piece):
    count = piece.shape[0]
    at = slice(number * count, (number + 1) * count)
    k_ref[at, :HD] = piece[:, :HD]
    k_ref[at, HD:] = piece[:, :HD]
    vt_ref[:HD, at] = jnp.transpose(piece[:, HD:], (1, 0))
    vt_ref[HD:, at] = (iota((vt_ref.shape[0] - HD, count), 0) == 0).astype(jnp.bfloat16)


def keys_kernel(first, parts, own_ref, *refs):
    k_ref, vt_ref = refs[-2:]
    store_keys(k_ref, vt_ref, first, own_ref[...])
    store_keys(k_ref, vt_ref, first + 1, jnp.concatenate([ref[...] for ref in refs[:parts]], axis=0))


def flash_kernel(far, chips, piece, me_ref, len_ref, pq_ref, k_ref, vt_ref, *refs):
    if far:
        before_ref, out_ref, q_ref, acc_ref, row_ref, s_ref, top_ref, job_ref, info_ref = refs
        acc_ref[...] = before_ref[...]
    else:
        acc_ref, q_ref, row_ref, s_ref, job_ref, info_ref = refs
        acc_ref[...] = jnp.zeros_like(acc_ref)
    width = TILE * H
    tiles = pq_ref.shape[0] // TILE
    all_width = tiles * width
    pieces = 4
    length = len_ref[me_ref[1]]
    chip, core = me_ref[0] // 2, lax.rem(me_ref[0], 2)
    for k in range(pieces):
        number = jnp.where(core == k // 2, 0, 2) + k % 2
        for base, at in ((0, chip), (2 * pieces, lax.rem(chip + chips // 2, chips))):
            info_ref[base + k] = at * (4 * piece) + piece * k
            info_ref[base + pieces + k] = number + base // 2
    base = 2 * pieces if far else 0
    meta = pq_ref[:, WIDE:].astype(jnp.float32)
    pos = meta[:, 0:1] * 256.0 + meta[:, 1:2] - 1.0
    last = jnp.minimum(pos, (length - 1).astype(jnp.float32))
    tops, lows = [], []
    for j in range(tiles):
        tops.append(last[j * TILE, 0].astype(jnp.int32))
        lows.append(last[(j + 1) * TILE - 1, 0].astype(jnp.int32))
    for j in range(tiles):
        here = last[j * TILE : (j + 1) * TILE]
        row_ref[0:1, j * width : (j + 1) * width] = jnp.concatenate([row_of(here)] * H, axis=1)
        rows = slice(j * TILE, (j + 1) * TILE)
        for h in range(H):
            x = pq_ref[rows, h * HD : (h + 1) * HD].astype(jnp.float32) * EXP_SCALE
            high = x.astype(jnp.bfloat16)
            at = slice(j * width + h * TILE, j * width + (h + 1) * TILE)
            q_ref[at, :HD] = high
            q_ref[at, HD:] = (x - high.astype(jnp.float32)).astype(jnp.bfloat16)
    count, whole = jnp.int32(0), []
    for j in range(tiles):
        for i in range(pieces):
            whole.append(info_ref[base + i] + (piece - 1) <= lows[j])
            job_ref[count] = j * pieces + i
            count += whole[-1].astype(jnp.int32)
    whole_turns = count // 2
    for j in range(tiles):
        for i in range(pieces):
            job_ref[count] = j * pieces + i
            count += ((info_ref[base + i] <= tops[j]) & jnp.logical_not(whole[j * pieces + i])).astype(jnp.int32)
    for k in range(3):
        job_ref[count + k] = tiles * pieces
    row_ref[0:1, all_width:] = jnp.full((1, width), -1.0, jnp.float32)
    q_ref[all_width:, :] = jnp.zeros((width, 2 * HD), jnp.bfloat16)

    def place(job):
        tile = job // pieces
        return pl.ds(pl.multiple_of(tile * width, width), width), job - tile * pieces + base

    def keys(c, a, n):
        return pl.ds(pl.multiple_of(info_ref[c + pieces] * piece + a, 128), n)

    def scores(cols, c, a, n):
        return dot(k_ref[keys(c, a, n), :], q_ref[cols, :], NT)

    def masked(s, cols, c, a):
        limit = row_ref[0:1, cols].astype(jnp.int32) - (info_ref[c] + a)
        return jnp.where(iota(s.shape, 0) <= limit, s, LOW)

    subs = [(0, SUB), (SUB, piece - SUB)]

    @pl.when(count > 0)
    def _():
        for k in range(2):
            cols, c = place(job_ref[k])
            s_ref[k] = scores(cols, c, *subs[0])

    def turn(b, mask):
        now = [place(job_ref[2 * b + k]) for k in range(2)]
        later = [place(job_ref[2 * b + 2 + k]) for k in range(2)]
        s = [s_ref[k] for k in range(2)]
        totals = [None, None]
        for i, (a, n) in enumerate(subs):
            if i + 1 < len(subs):
                next_s = [scores(cols, c, *subs[i + 1]) for cols, c in now]
            else:
                next_s = [scores(cols, c, *subs[0]) for cols, c in later]
            for k, (cols, c) in enumerate(now):
                weights = jnp.exp2(masked(s[k], cols, c, a) if mask else s[k]).astype(jnp.bfloat16)
                term = dot(vt_ref[:, keys(c, a, n)], weights)
                totals[k] = term if totals[k] is None else totals[k] + term
            s = next_s
        for k in range(2):
            s_ref[k] = s[k]
        for k, (cols, _) in enumerate(now):
            acc_ref[:, cols] += totals[k]

    pl.loop(0, whole_turns)(lambda b: turn(b, False))
    pl.loop(whole_turns, (count + 1) // 2)(lambda b: turn(b, True))
    if not far:
        return
    top_ref[0:1, :] = jnp.zeros((1, all_width), jnp.float32)
    total = acc_ref[HD : HD + 1, :all_width]
    dead = row_ref[0:1, :all_width] < jnp.minimum(info_ref[0], info_ref[base]).astype(jnp.float32)
    fine = dead | ((total > 2.0**-60) & (total < 2.0**100))

    @pl.when(jnp.logical_not(jnp.min(fine.astype(jnp.float32)) > 0.5))
    def _():
        acc_ref[...] = jnp.zeros_like(acc_ref)
        top_ref[0:1, :] = jnp.full((1, all_width), 0.1 * LOW, jnp.float32)

        def careful(i, carry):
            chunks = piece // 128
            cols = pl.ds(pl.multiple_of(i // (2 * pieces * chunks) * width, width), width)
            c, a = i // chunks % (2 * pieces), i % chunks * 128
            c += jnp.where(c < pieces, 0, pieces)
            s = masked(scores(cols, c, a, 128), cols, c, a)
            before = top_ref[0:1, cols]
            after = jnp.maximum(before, jnp.max(s, axis=0, keepdims=True))
            weights = jnp.exp2(s - after).astype(jnp.bfloat16)
            acc_ref[:, cols] = acc_ref[:, cols] * jnp.exp2(before - after) + dot(vt_ref[:, keys(c, a, 128)], weights)
            top_ref[0:1, cols] = after
            return carry

        lax.fori_loop(0, tiles * 2 * pieces * (piece // 128), careful, 0)

    total = acc_ref[HD : HD + 1, :all_width]
    some = total > 0.0
    safe = jnp.where(some, total, 1.0)
    out_ref[:HD, :] = (acc_ref[:HD, :all_width] * (1.0 / safe)).astype(jnp.bfloat16)
    lse = jnp.where(some, top_ref[0:1, :] + jnp.log2(safe), LOW)
    a = lse.astype(jnp.bfloat16).astype(jnp.float32)
    b = (lse - a).astype(jnp.bfloat16).astype(jnp.float32)
    row = iota((OUT_ROWS - HD, all_width), 0)
    terms = jnp.where(row == 0, a, jnp.where(row == 1, b, jnp.where(row == 2, lse - a - b, 0.0)))
    out_ref[HD:, :] = terms.astype(jnp.bfloat16)


def merge_kernel(cuts, *refs):
    count = sum(cuts)
    pieces, back_ref, outs, slot_ref = list(refs[:count]), refs[count], refs[count + 1 : -1], refs[-1]
    fold = back_ref.shape[0]
    width = TILE * H
    parts = []
    for cut in cuts:
        taken, pieces = pieces[:cut], pieces[cut:]
        parts.append([(ref, slice(i, i + width)) for ref in taken for i in range(0, ref.shape[1], width)])
    for j in range(slot_ref.shape[0] // TILE):
        here = [part[j] for part in parts]
        lses = [sum(part[HD + i : HD + i + 1, cols].astype(jnp.float32) for i in range(3)) for part, cols in here]
        high = functools.reduce(jnp.maximum, lses)
        shares = [jnp.exp2(lse - high) for lse in lses]
        scale = 1.0 / functools.reduce(jnp.add, shares)
        merged = sum((share * scale) * part[:HD, cols].astype(jnp.float32) for share, (part, cols) in zip(shares, here))
        merged = jnp.transpose(merged, (1, 0)).astype(jnp.bfloat16)
        for h in range(H):
            slot_ref[j * TILE : (j + 1) * TILE, h * HD : (h + 1) * HD] = merged[h * TILE : (h + 1) * TILE]
    block, cut = outs[0].shape
    placed = sum(dot(back_ref[f], slot_ref[:, f * cut : (f + 1) * cut]) for f in range(fold))
    placed = placed.astype(jnp.bfloat16)
    for d, out in enumerate(outs):
        out[...] = placed[d * block : (d + 1) * block]


def unroute_kernel(*refs):
    blocks, back_ref, out = refs[:-2], refs[-2], refs[-1]
    width = blocks[0].shape[1]
    joined = jnp.concatenate([b[...] for b in reversed(blocks)], axis=0)
    for f in range(back_ref.shape[0]):
        out[:, f * width : (f + 1) * width] = dot(back_ref[f], joined).astype(jnp.bfloat16)


def swapped(block, axis, distance):
    devices = range(lax.axis_size(axis))
    return lax.ppermute(block, axis, [(i, i ^ distance) for i in devices])


def per_device(queries, q_pos, req_of, cache, cache_len):
    tok_rows = queries.shape[0]
    groups = lax.axis_size("req")
    cycle = lax.axis_size("ctx")
    chips = cycle // 2
    capacity = 5 * tok_rows // (4 * groups)
    slots = groups * capacity
    fold = fold_of(capacity)
    block, width = capacity * fold, WIDE // fold
    shard_len = cache.shape[1]
    half = shard_len // 2
    here = lax.axis_index("ctx")
    mine = lax.axis_index("req")
    me = jnp.stack([here, mine]).astype(jnp.int32)
    bf = lambda *shape: jax.ShapeDtypeStruct(shape, jnp.bfloat16)

    *sends, back_tok, shard = call(
        functools.partial(route_kernel, capacity),
        [bf(block, width + META)] * groups + [bf(fold, tok_rows, groups * block)] + [bf(shard_len, 2 * HD)],
        [SMEM] + [pl.BlockSpec(memory_space=pltpu.HBM)] * 4,
        "route",
        scratch=[
            pltpu.VMEM((1, tok_rows), jnp.int32),
            pltpu.VMEM((1, tok_rows), jnp.int32),
            pltpu.VMEM((tok_rows, WIDE), jnp.bfloat16),
            pltpu.SemaphoreType.DMA((4,)),
        ],
    )(me, *[in_hbm(x) for x in (req_of.reshape(1, tok_rows), q_pos.reshape(1, tok_rows), queries, cache[0])])
    blocks = {d: swapped(sends[d], "req", d) for d in reversed(range(1, groups))}
    blocks[0] = sends[0]
    far_shard = swapped(shard, "ctx", cycle // 2)
    sibling = swapped(shard, "ctx", 1)
    all_keys = [bf(4 * shard_len, 2 * HD), bf(HD + 16, 4 * shard_len)]
    keys = call(functools.partial(keys_kernel, 0, 1), all_keys, [VMEM] * 2, "home_keys")(shard, sibling)
    blocks[0], *keys = lax.optimization_barrier((blocks[0], *keys))

    sorted_q, back_slot = call(
        functools.partial(sort_kernel, capacity),
        [bf(slots, WIDE + META), bf(fold, groups * block, slots)],
        [VMEM] * groups,
        "sort",
    )(*[blocks[d] for d in reversed(range(groups))])
    visiting = {d: swapped(sorted_q, "ctx", 2 * d) for d in range(1, chips // 2)}

    def flash(q, keys, before=None):
        far = before is not None
        extra = (slots + TILE) * H
        sums = jax.ShapeDtypeStruct((HD + 16, extra), jnp.float32)
        scratch = [
            pltpu.VMEM((extra, 2 * HD), jnp.bfloat16),
            pltpu.VMEM(sums.shape, sums.dtype),
            pltpu.VMEM((8, extra), jnp.float32),
            pltpu.VMEM((2, SUB, TILE * H), jnp.float32),
            pltpu.VMEM((8, slots * H), jnp.float32),
            pltpu.SMEM((4 * slots // TILE + 4,), jnp.int32),
            pltpu.SMEM((16,), jnp.int32),
        ]
        return call(
            functools.partial(flash_kernel, far, chips, half),
            bf(OUT_ROWS, slots * H) if far else sums,
            [SMEM, SMEM] + [VMEM] * (4 if far else 3),
            "flash_far" if far else "flash_home",
            scratch=scratch if far else [scratch[i] for i in (0, 2, 3, 5, 6)],
        )(me, cache_len, q, *keys, *([before] if far else []))

    turn = flash(sorted_q, keys)
    sums = {0: turn}
    for d in visiting:
        turn, visiting[d] = lax.optimization_barrier((turn, visiting[d]))
        turn = sums[d] = flash(visiting[d], keys)
    turn, far_shard, *keys = lax.optimization_barrier((turn, far_shard, *keys))
    far_sibling = [swapped(far_shard[i * half : (i + 1) * half], "ctx", 1) for i in range(2)]
    keys = call(
        functools.partial(keys_kernel, 2, 2), all_keys, [VMEM] * 5, "far_keys", aliases={3: 0, 4: 1}
    )(far_shard, *far_sibling, *keys)
    home = []
    for d in visiting:
        turn, q = lax.optimization_barrier((turn, visiting[d]))
        turn = flash(q, keys, sums[d])
        home.append(swapped(turn, "ctx", 2 * d))
    turn, q = lax.optimization_barrier((turn, sorted_q))
    home.append(flash(q, keys, sums[0]))
    cuts = (1,) * len(home)
    outs = call(
        functools.partial(merge_kernel, cuts),
        [bf(block, width)] * groups,
        [VMEM] * (len(home) + 1),
        "merge",
        scratch=[pltpu.VMEM((slots, WIDE), jnp.bfloat16)],
    )(*home, back_slot)
    back = [swapped(outs[d], "req", d) for d in reversed(range(1, groups))] + [outs[0]]
    return call(unroute_kernel, bf(tok_rows, WIDE), [VMEM] * (groups + 1), "unroute")(*back, back_tok)


def solution(mesh):
    in_specs = (
        P(("ctx", "req"), None),
        P(("ctx", "req")),
        P(("ctx", "req"), None),
        P("req", "ctx", None),
        P(),
    )
    out_specs = P(("ctx", "req"), None)
    return jax.shard_map(
        per_device, mesh=mesh, in_specs=in_specs, out_specs=out_specs, check_vma=False
    )
```

```python
import functools
import math

import jax
import jax.numpy as jnp
from jax import lax
from jax.experimental import pallas as pl
from jax.experimental.pallas import tpu as pltpu
from jax.sharding import PartitionSpec as P

H = 16
HD = 128
WIDE = H * HD
META = 128
LOW = -1e30
TILE = 16
SUB = 256
OUT_ROWS = HD + 8
EXP_SCALE = HD**-0.5 * math.log2(math.e)
NT = (((1,), (1,)), ((), ()))
NN = (((1,), (0,)), ((), ()))
VMEM = pl.BlockSpec(memory_space=pltpu.VMEM)
SMEM = pl.BlockSpec(memory_space=pltpu.SMEM)


def dot(a, b, dims=NN):
    return lax.dot_general(a, b, dims, preferred_element_type=jnp.float32)


def in_hbm(x):
    return pltpu.with_memory_space_constraint(x, pltpu.HBM)


def iota(shape, dim):
    return lax.broadcasted_iota(jnp.int32, shape, dim)


def row_of(column):
    return jnp.transpose(jnp.broadcast_to(column, (column.shape[0], 128)), (1, 0))[:1, :]


def call(body, out_shape, in_specs, name, scratch=(), limit=20, aliases=None):
    many = isinstance(out_shape, list)
    return pl.pallas_call(
        body,
        out_shape=out_shape,
        in_specs=in_specs,
        out_specs=[VMEM] * len(out_shape) if many else VMEM,
        scratch_shapes=list(scratch),
        compiler_params=pltpu.CompilerParams(vmem_limit_bytes=limit << 20),
        cost_estimate=pl.CostEstimate(flops=1, bytes_accessed=1, transcendentals=0),
        input_output_aliases=aliases or {},
        name=name,
    )


def fold_of(capacity):
    fold = 1
    while capacity * fold % 8:
        fold *= 2
    return fold


def route_kernel(capacity, me_ref, req_hbm, pos_hbm, q_hbm, shard_hbm, *outs):
    outs, (req_ref, pos_ref, q_ref, sem) = outs[:-4], outs[-4:]
    sends, back_ref, shard_ref = outs[:-2], outs[-2], outs[-1]
    moves = [(req_hbm, req_ref), (pos_hbm, pos_ref), (q_hbm, q_ref), (shard_hbm, shard_ref)]
    fetches = [pltpu.make_async_copy(src, dst, sem.at[i]) for i, (src, dst) in enumerate(moves)]
    for fetch in fetches:
        fetch.start()
    for fetch in fetches[:3]:
        fetch.wait()
    rows = q_ref.shape[0]
    fold = fold_of(capacity)
    block, width = capacity * fold, WIDE // fold
    i0, i1 = iota((rows, rows), 0), iota((rows, rows), 1)
    target_r = req_ref[...]
    target_c = jnp.sum(jnp.where(i0 == i1, target_r, 0), axis=1, keepdims=True)
    same = target_c == target_r
    rank_c = jnp.sum((same & (i1 < i0)).astype(jnp.int32), axis=1, keepdims=True)
    rank_r = jnp.sum((same & (i0 < i1)).astype(jnp.int32), axis=0, keepdims=True)
    slot_c = (target_c ^ me_ref[1]) * block + rank_c
    slot_r = (target_r ^ me_ref[1]) * block + rank_r
    total = len(sends) * block
    moved = jnp.zeros((total, width), jnp.float32)
    taken = jnp.zeros((total, rows), jnp.float32)
    for f in range(fold):
        back_ref[f] = (slot_c + f * capacity == iota((rows, total), 1)).astype(jnp.bfloat16)
        place = (slot_r + f * capacity == iota((total, rows), 0)).astype(jnp.float32)
        moved += dot(place.astype(jnp.bfloat16), q_ref[:, f * width : (f + 1) * width])
        taken += place
    plus = pos_ref[...] + 1
    high = jnp.sum(taken * (plus >> 8).astype(jnp.float32), axis=1, keepdims=True)
    low = jnp.sum(taken * (plus & 255).astype(jnp.float32), axis=1, keepdims=True)
    lane = iota((total, META), 1)
    meta = jnp.where(lane == 0, high, jnp.where(lane == 1, low, 0.0)).astype(jnp.bfloat16)
    moved = moved.astype(jnp.bfloat16)
    for d, out in enumerate(sends):
        out[:, :width] = moved[d * block : (d + 1) * block]
        out[:, width:] = meta[d * block : (d + 1) * block]
    for fetch in fetches[3:]:
        fetch.wait()


def row_parts(shape, dim, capacity):
    fold = fold_of(capacity)
    row = iota(shape, dim)
    token = jnp.zeros(shape, jnp.int32)
    part = jnp.zeros(shape, jnp.int32)
    for i in range(1, shape[dim] // capacity):
        passed = (row >= i * capacity).astype(jnp.int32)
        part += passed if i % fold else (1 - fold) * passed
    token = row - part * capacity
    for i in range(1, shape[dim] // (capacity * fold)):
        token -= (row >= i * capacity * fold).astype(jnp.int32) * (capacity * fold - capacity)
    return token, part


def sort_kernel(capacity, *refs):
    blocks, out, back_ref = refs[:-2], refs[-2], refs[-1]
    slots = out.shape[0]
    fold = fold_of(capacity)
    width = WIDE // fold
    joined = jnp.concatenate([b[...] for b in reversed(blocks)], axis=0)
    total = joined.shape[0]
    meta = joined[:, width:].astype(jnp.float32)
    pos_c = meta[:, 0:1] * 256.0 + meta[:, 1:2]
    pos_r = row_of(pos_c)
    token_c, part_c = row_parts((total, 1), 0, capacity)
    token_r, part_r = row_parts((1, total), 1, capacity)
    ahead_r = ((pos_c > pos_r) | ((pos_c == pos_r) & (token_c < token_r))) & (part_c == 0)
    ahead_c = ((pos_r > pos_c) | ((pos_r == pos_c) & (token_r < token_c))) & (part_r == 0)
    rank_r = jnp.sum(ahead_r.astype(jnp.int32), axis=0, keepdims=True)
    rank_c = jnp.sum(ahead_c.astype(jnp.int32), axis=1, keepdims=True)
    place = rank_r == iota((slots, total), 0)
    for f in range(fold):
        mine = (place & (part_r == f)).astype(jnp.bfloat16)
        out[:, f * width : (f + 1) * width] = dot(mine, joined[:, :width]).astype(jnp.bfloat16)
        if f == 0:
            out[:, WIDE:] = dot(mine, joined[:, width:]).astype(jnp.bfloat16)
        back_ref[f] = ((rank_c == iota((total, slots), 1)) & (part_c == f)).astype(jnp.bfloat16)


def store_keys(k_ref, vt_ref, number, piece):
    count = piece.shape[0]
    at = slice(number * count, (number + 1) * count)
    k_ref[at, :HD] = piece[:, :HD]
    k_ref[at, HD:] = piece[:, :HD]
    vt_ref[:HD, at] = jnp.transpose(piece[:, HD:], (1, 0))


def keys_kernel(first, parts, own_ref, *refs):
    k_ref, vt_ref = refs[-2:]
    store_keys(k_ref, vt_ref, first, own_ref[...])
    store_keys(k_ref, vt_ref, first + 1, jnp.concatenate([ref[...] for ref in refs[:parts]], axis=0))


def flash_kernel(far, chips, piece, me_ref, len_ref, pq_ref, k_ref, vt_ref, *refs):
    if far:
        before_ref, out_ref, q_ref, acc_ref, row_ref, s_ref, top_ref, job_ref, info_ref = refs
        acc_ref[...] = before_ref[...]
    else:
        acc_ref, q_ref, row_ref, s_ref, job_ref, info_ref = refs
        acc_ref[...] = jnp.zeros_like(acc_ref)
    width = TILE * H
    tiles = pq_ref.shape[0] // TILE
    all_width = tiles * width
    pieces = 4
    length = len_ref[me_ref[1]]
    chip, core = me_ref[0] // 2, lax.rem(me_ref[0], 2)
    for k in range(pieces):
        number = jnp.where(core == k // 2, 0, 2) + k % 2
        for base, at in ((0, chip), (2 * pieces, lax.rem(chip + chips // 2, chips))):
            info_ref[base + k] = at * (4 * piece) + piece * k
            info_ref[base + pieces + k] = number + base // 2
    base = 2 * pieces if far else 0
    meta = pq_ref[:, WIDE:].astype(jnp.float32)
    pos = meta[:, 0:1] * 256.0 + meta[:, 1:2] - 1.0
    last = jnp.minimum(pos, (length - 1).astype(jnp.float32))
    tops, lows = [], []
    for j in range(tiles):
        tops.append(last[j * TILE, 0].astype(jnp.int32))
        lows.append(last[(j + 1) * TILE - 1, 0].astype(jnp.int32))
    for j in range(tiles):
        here = last[j * TILE : (j + 1) * TILE]
        row_ref[0:1, j * width : (j + 1) * width] = jnp.concatenate([row_of(here)] * H, axis=1)
        rows = slice(j * TILE, (j + 1) * TILE)
        for h in range(H):
            x = pq_ref[rows, h * HD : (h + 1) * HD].astype(jnp.float32) * EXP_SCALE
            high = x.astype(jnp.bfloat16)
            at = slice(j * width + h * TILE, j * width + (h + 1) * TILE)
            q_ref[at, :HD] = high
            q_ref[at, HD:] = (x - high.astype(jnp.float32)).astype(jnp.bfloat16)
    count, whole = jnp.int32(0), []
    for j in range(tiles):
        for i in range(pieces):
            whole.append(info_ref[base + i] + (piece - 1) <= lows[j])
            job_ref[count] = j * pieces + i
            count += whole[-1].astype(jnp.int32)
    whole_turns = count // 2
    for j in range(tiles):
        for i in range(pieces):
            job_ref[count] = j * pieces + i
            count += ((info_ref[base + i] <= tops[j]) & jnp.logical_not(whole[j * pieces + i])).astype(jnp.int32)
    for k in range(3):
        job_ref[count + k] = tiles * pieces
    row_ref[0:1, all_width:] = jnp.full((1, width), -1.0, jnp.float32)
    q_ref[all_width:, :] = jnp.zeros((width, 2 * HD), jnp.bfloat16)

    def place(job):
        tile = job // pieces
        return pl.ds(pl.multiple_of(tile * width, width), width), job - tile * pieces + base

    def keys(c, a, n):
        return pl.ds(pl.multiple_of(info_ref[c + pieces] * piece + a, 128), n)

    def scores(cols, c, a, n):
        return dot(k_ref[keys(c, a, n), :], q_ref[cols, :], NT)

    def masked(s, cols, c, a):
        limit = row_ref[0:1, cols].astype(jnp.int32) - (info_ref[c] + a)
        return jnp.where(iota(s.shape, 0) <= limit, s, LOW)

    subs = [(0, SUB), (SUB, piece - SUB)]

    @pl.when(count > 0)
    def _():
        for k in range(2):
            cols, c = place(job_ref[k])
            s_ref[k] = scores(cols, c, *subs[0])

    def turn(b, mask):
        now = [place(job_ref[2 * b + k]) for k in range(2)]
        later = [place(job_ref[2 * b + 2 + k]) for k in range(2)]
        s = [s_ref[k] for k in range(2)]
        totals, weight_sums = [None, None], [0.0, 0.0]
        for i, (a, n) in enumerate(subs):
            if i + 1 < len(subs):
                next_s = [scores(cols, c, *subs[i + 1]) for cols, c in now]
            else:
                next_s = [scores(cols, c, *subs[0]) for cols, c in later]
            for k, (cols, c) in enumerate(now):
                weights = jnp.exp2(masked(s[k], cols, c, a) if mask else s[k])
                weight_sums[k] += jnp.sum(weights, axis=0, keepdims=True)
                term = dot(vt_ref[:, keys(c, a, n)], weights.astype(jnp.bfloat16))
                totals[k] = term if totals[k] is None else totals[k] + term
            s = next_s
        for k in range(2):
            s_ref[k] = s[k]
        for k, (cols, _) in enumerate(now):
            acc_ref[:HD, cols] += totals[k]
            acc_ref[HD : HD + 1, cols] += weight_sums[k]

    pl.loop(0, whole_turns)(lambda b: turn(b, False))
    pl.loop(whole_turns, (count + 1) // 2)(lambda b: turn(b, True))
    if not far:
        return
    top_ref[0:1, :] = jnp.zeros((1, all_width), jnp.float32)
    total = acc_ref[HD : HD + 1, :all_width]
    dead = row_ref[0:1, :all_width] < jnp.minimum(info_ref[0], info_ref[base]).astype(jnp.float32)
    fine = dead | ((total > 2.0**-60) & (total < 2.0**100))

    @pl.when(jnp.logical_not(jnp.min(fine.astype(jnp.float32)) > 0.5))
    def _():
        acc_ref[...] = jnp.zeros_like(acc_ref)
        top_ref[0:1, :] = jnp.full((1, all_width), 0.1 * LOW, jnp.float32)

        def careful(i, carry):
            chunks = piece // 128
            cols = pl.ds(pl.multiple_of(i // (2 * pieces * chunks) * width, width), width)
            c, a = i // chunks % (2 * pieces), i % chunks * 128
            c += jnp.where(c < pieces, 0, pieces)
            s = masked(scores(cols, c, a, 128), cols, c, a)
            before = top_ref[0:1, cols]
            after = jnp.maximum(before, jnp.max(s, axis=0, keepdims=True))
            weights = jnp.exp2(s - after)
            shrink = jnp.exp2(before - after)
            term = dot(vt_ref[:, keys(c, a, 128)], weights.astype(jnp.bfloat16))
            acc_ref[:HD, cols] = acc_ref[:HD, cols] * shrink + term
            acc_ref[HD : HD + 1, cols] = acc_ref[HD : HD + 1, cols] * shrink + jnp.sum(weights, axis=0, keepdims=True)
            top_ref[0:1, cols] = after
            return carry

        lax.fori_loop(0, tiles * 2 * pieces * (piece // 128), careful, 0)

    total = acc_ref[HD : HD + 1, :all_width]
    some = total > 0.0
    safe = jnp.where(some, total, 1.0)
    out_ref[:HD, :] = (acc_ref[:HD, :all_width] * (1.0 / safe)).astype(jnp.bfloat16)
    lse = jnp.where(some, top_ref[0:1, :] + jnp.log2(safe), LOW)
    a = lse.astype(jnp.bfloat16).astype(jnp.float32)
    b = (lse - a).astype(jnp.bfloat16).astype(jnp.float32)
    row = iota((OUT_ROWS - HD, all_width), 0)
    terms = jnp.where(row == 0, a, jnp.where(row == 1, b, jnp.where(row == 2, lse - a - b, 0.0)))
    out_ref[HD:, :] = terms.astype(jnp.bfloat16)


def merge_kernel(cuts, *refs):
    count = sum(cuts)
    pieces, back_ref, outs, slot_ref = list(refs[:count]), refs[count], refs[count + 1 : -1], refs[-1]
    fold = back_ref.shape[0]
    width = TILE * H
    parts = []
    for cut in cuts:
        taken, pieces = pieces[:cut], pieces[cut:]
        parts.append([(ref, slice(i, i + width)) for ref in taken for i in range(0, ref.shape[1], width)])
    for j in range(slot_ref.shape[0] // TILE):
        here = [part[j] for part in parts]
        lses = [sum(part[HD + i : HD + i + 1, cols].astype(jnp.float32) for i in range(3)) for part, cols in here]
        high = functools.reduce(jnp.maximum, lses)
        shares = [jnp.exp2(lse - high) for lse in lses]
        scale = 1.0 / functools.reduce(jnp.add, shares)
        merged = sum((share * scale) * part[:HD, cols].astype(jnp.float32) for share, (part, cols) in zip(shares, here))
        merged = jnp.transpose(merged, (1, 0)).astype(jnp.bfloat16)
        for h in range(H):
            slot_ref[j * TILE : (j + 1) * TILE, h * HD : (h + 1) * HD] = merged[h * TILE : (h + 1) * TILE]
    block, cut = outs[0].shape
    placed = sum(dot(back_ref[f], slot_ref[:, f * cut : (f + 1) * cut]) for f in range(fold))
    placed = placed.astype(jnp.bfloat16)
    for d, out in enumerate(outs):
        out[...] = placed[d * block : (d + 1) * block]


def unroute_kernel(*refs):
    blocks, back_ref, out = refs[:-2], refs[-2], refs[-1]
    width = blocks[0].shape[1]
    joined = jnp.concatenate([b[...] for b in reversed(blocks)], axis=0)
    for f in range(back_ref.shape[0]):
        out[:, f * width : (f + 1) * width] = dot(back_ref[f], joined).astype(jnp.bfloat16)


def swapped(block, axis, distance):
    devices = range(lax.axis_size(axis))
    return lax.ppermute(block, axis, [(i, i ^ distance) for i in devices])


def per_device(queries, q_pos, req_of, cache, cache_len):
    tok_rows = queries.shape[0]
    groups = lax.axis_size("req")
    cycle = lax.axis_size("ctx")
    chips = cycle // 2
    capacity = 5 * tok_rows // (4 * groups)
    slots = groups * capacity
    fold = fold_of(capacity)
    block, width = capacity * fold, WIDE // fold
    shard_len = cache.shape[1]
    half = shard_len // 2
    here = lax.axis_index("ctx")
    mine = lax.axis_index("req")
    me = jnp.stack([here, mine]).astype(jnp.int32)
    bf = lambda *shape: jax.ShapeDtypeStruct(shape, jnp.bfloat16)

    *sends, back_tok, shard = call(
        functools.partial(route_kernel, capacity),
        [bf(block, width + META)] * groups + [bf(fold, tok_rows, groups * block)] + [bf(shard_len, 2 * HD)],
        [SMEM] + [pl.BlockSpec(memory_space=pltpu.HBM)] * 4,
        "route",
        scratch=[
            pltpu.VMEM((1, tok_rows), jnp.int32),
            pltpu.VMEM((1, tok_rows), jnp.int32),
            pltpu.VMEM((tok_rows, WIDE), jnp.bfloat16),
            pltpu.SemaphoreType.DMA((4,)),
        ],
    )(me, *[in_hbm(x) for x in (req_of.reshape(1, tok_rows), q_pos.reshape(1, tok_rows), queries, cache[0])])
    blocks = {d: swapped(sends[d], "req", d) for d in reversed(range(1, groups))}
    blocks[0] = sends[0]
    far_shard = swapped(shard, "ctx", cycle // 2)
    sibling = swapped(shard, "ctx", 1)
    all_keys = [bf(4 * shard_len, 2 * HD), bf(HD, 4 * shard_len)]
    keys = call(functools.partial(keys_kernel, 0, 1), all_keys, [VMEM] * 2, "home_keys")(shard, sibling)
    blocks[0], *keys = lax.optimization_barrier((blocks[0], *keys))

    sorted_q, back_slot = call(
        functools.partial(sort_kernel, capacity),
        [bf(slots, WIDE + META), bf(fold, groups * block, slots)],
        [VMEM] * groups,
        "sort",
    )(*[blocks[d] for d in reversed(range(groups))])
    visiting = {d: swapped(sorted_q, "ctx", 2 * d) for d in range(1, chips // 2)}

    def flash(q, keys, before=None):
        far = before is not None
        extra = (slots + TILE) * H
        sums = jax.ShapeDtypeStruct((HD + 8, extra), jnp.float32)
        scratch = [
            pltpu.VMEM((extra, 2 * HD), jnp.bfloat16),
            pltpu.VMEM(sums.shape, sums.dtype),
            pltpu.VMEM((8, extra), jnp.float32),
            pltpu.VMEM((2, SUB, TILE * H), jnp.float32),
            pltpu.VMEM((8, slots * H), jnp.float32),
            pltpu.SMEM((4 * slots // TILE + 4,), jnp.int32),
            pltpu.SMEM((16,), jnp.int32),
        ]
        return call(
            functools.partial(flash_kernel, far, chips, half),
            bf(OUT_ROWS, slots * H) if far else sums,
            [SMEM, SMEM] + [VMEM] * (4 if far else 3),
            "flash_far" if far else "flash_home",
            scratch=scratch if far else [scratch[i] for i in (0, 2, 3, 5, 6)],
        )(me, cache_len, q, *keys, *([before] if far else []))

    turn = flash(sorted_q, keys)
    sums = {0: turn}
    for d in visiting:
        turn, visiting[d] = lax.optimization_barrier((turn, visiting[d]))
        turn = sums[d] = flash(visiting[d], keys)
    turn, far_shard, *keys = lax.optimization_barrier((turn, far_shard, *keys))
    far_sibling = [swapped(far_shard[i * half : (i + 1) * half], "ctx", 1) for i in range(2)]
    keys = call(
        functools.partial(keys_kernel, 2, 2), all_keys, [VMEM] * 5, "far_keys", aliases={3: 0, 4: 1}
    )(far_shard, *far_sibling, *keys)
    home = []
    for d in visiting:
        turn, q = lax.optimization_barrier((turn, visiting[d]))
        turn = flash(q, keys, sums[d])
        home.append(swapped(turn, "ctx", 2 * d))
    turn, q = lax.optimization_barrier((turn, sorted_q))
    home.append(flash(q, keys, sums[0]))
    cuts = (1,) * len(home)
    outs = call(
        functools.partial(merge_kernel, cuts),
        [bf(block, width)] * groups,
        [VMEM] * (len(home) + 1),
        "merge",
        scratch=[pltpu.VMEM((slots, WIDE), jnp.bfloat16)],
    )(*home, back_slot)
    back = [swapped(outs[d], "req", d) for d in reversed(range(1, groups))] + [outs[0]]
    return call(unroute_kernel, bf(tok_rows, WIDE), [VMEM] * (groups + 1), "unroute")(*back, back_tok)


def solution(mesh):
    in_specs = (
        P(("ctx", "req"), None),
        P(("ctx", "req")),
        P(("ctx", "req"), None),
        P("req", "ctx", None),
        P(),
    )
    out_specs = P(("ctx", "req"), None)
    return jax.shard_map(
        per_device, mesh=mesh, in_specs=in_specs, out_specs=out_specs, check_vma=False
    )
```
